512 devices in a mesh: lag: 64 (over y, x, core), row: 8 (over z).
Axes of the slice: x: 4, y: 8, z: 8, core: 2. Of those that a mesh axis runs over, the one named last changes fastest.
Arguments:
- blocks: bfloat16 [128, 2048, 2048], P('lag', 'row'), may hold values from -0.03125 to 0.03125
- history: bfloat16 [128, 2048, 128], P('lag'), may hold values from -6 to 6
- excitation: float32 [2, 2048, 128], P(None, 'row'), may hold values from -6 to 6
- self_inverse: float32 [2048, 2048], P('lag', 'row'), may hold values from -2 to 2
Outputs:
- currents: float32 [2, 2048, 128], P(None, 'lag')
The draws below stay inside these ranges and needn't reach their ends.
All inputs are finite; a program needn't handle non-finite values.
Results may differ from the reference program's by a relative error of at most 0.0003.
Values may be sent and summed in bfloat16 or wider, within the bound.
No kernel may reach another device: no remote copies, remote signals or barrier semaphores. Data moves between devices by JAX's collectives and lax.ppermute only.
A program may use at most 64 MiB of HBM per device.

```python
import math
import jax
import jax.numpy as jnp
from jax import lax

P_SIZE = 2048
COLUMNS = 128
STEPS = 2
LAGS = 128


def draw_self_inverse(key, part):
    first, second = jax.random.split(jax.random.fold_in(key, 11))
    diagonal = jnp.exp(jax.random.uniform(first, (P_SIZE,), jnp.float32, math.log(0.5), math.log(1.8)))
    spread = jnp.clip(jax.random.normal(second, (P_SIZE, P_SIZE), jnp.float32), -4.0, 4.0)
    return spread * (0.6 / math.sqrt(P_SIZE)) + jnp.diag(diagonal)


def spiked(drawn, own_key, source, target, shards_of, factor):
    owner, partner = [(jnp.arange(drawn.shape[position]) // (drawn.shape[position] // shards_of)).reshape([-1 if axis == position else 1 for axis in range(drawn.ndim)]) for position in (source, target)]
    chosen = jax.random.permutation(own_key, shards_of)[partner]
    strong = (owner == chosen) | (owner == (partner + shards_of // 2) % shards_of)
    return jnp.where(strong, factor * drawn, drawn)


def level_of(rng, dims, shards, least, largest):
    def one(dim, shards_of):
        draws = jax.random.uniform(jax.random.fold_in(jax.random.fold_in(rng, 6), dim), (shards_of,), jnp.float32, least / len(shards), largest / len(shards))
        return jnp.repeat(jnp.exp(draws), dims[dim] // shards_of).reshape((-1,) + (1,) * (len(dims) - dim - 1))

    factor_of = one(*shards[0])
    for cut in shards[1:]:
        factor_of = factor_of * one(*cut)
    return factor_of


def gaussian(stream_key, shape, deviation, bound, cuts=(), held_as=jnp.bfloat16):
    entries = deviation * jax.random.normal(stream_key, shape, jnp.float32)
    if cuts:
        entries = entries * level_of(stream_key, shape, cuts, -0.22, 0.18)
    return jnp.clip(entries, -bound, bound).astype(held_as)


def gaussian_with(stream_key, extent, scale, bound, pieces, heavy, kind=jnp.bfloat16):
    result = scale * jax.random.normal(stream_key, extent, jnp.float32)
    if pieces:
        result = result * level_of(stream_key, extent, pieces, -0.22, 0.18)
    return jnp.clip(spiked(result, jax.random.fold_in(stream_key, 3), *heavy), -bound, bound).astype(kind)


def setup_inputs(seed: int = 0) -> dict:
    key_of = jax.random.split(jax.random.key(seed), 5)
    return {
        "blocks": gaussian_with(key_of[0], (LAGS, P_SIZE, P_SIZE), (P_SIZE * LAGS) ** -0.5, 0.03125, ((0, 64), (1, 8)), (0, 1, 64, 4.0)),
        "history": gaussian(key_of[1], (LAGS, P_SIZE, COLUMNS), 1.0, 6.0, ((0, 64),)),
        "excitation": gaussian(key_of[2], (STEPS, P_SIZE, COLUMNS), 1.0, 6.0, ((1, 8),), jnp.float32),
        "self_inverse": draw_self_inverse(jax.random.fold_in(key_of[4], 71), 0),
    }


def lag_total(blocks, past):
    def add_lag(total, pair):
        return total + jnp.dot(pair[0], pair[1], preferred_element_type=jnp.float32), None

    start = jnp.zeros((blocks.shape[1], past.shape[2]), jnp.float32)
    return lax.scan(add_lag, start, (blocks, past))[0]


def reference(blocks, history, excitation, self_inverse):
    past = history
    results = []
    for marker in range(STEPS):
        summed = lag_total(blocks, past)
        residual = excitation[marker] - summed
        current = jnp.dot(self_inverse, residual, precision=lax.Precision.HIGHEST, preferred_element_type=jnp.float32)
        results.append(current)
        past = jnp.concatenate([current.astype(jnp.bfloat16)[None], past[:-1]], axis=0)
    return jnp.stack(results)
```

```python
import numpy as np
import jax
import jax.numpy as jnp
from jax import lax
from jax.sharding import Mesh, PartitionSpec as P

LAG = ("y", "x", "core")
W = ("x", "core")
F32 = jnp.float32


def exchange(array, axes):
    n = lax.axis_size(axes)
    copies = jnp.broadcast_to(array, (n, *array.shape))
    return lax.all_to_all(copies, axes, 0, 0, tiled=True)


def all_sum(array, axes):
    return jnp.sum(exchange(array, axes), axis=0)


def scatter_sum(pieces, axes):
    return jnp.sum(lax.all_to_all(pieces, axes, 0, 0, tiled=True), axis=0)


def times(left, right, precision=None):
    return lax.dot_general(
        left, right, (((1,), (1,)), ((), ())), precision=precision, preferred_element_type=F32
    )


def shards(blocks, history, excitation, self_inverse):
    ny, nw, nz = lax.axis_size("y"), lax.axis_size(W), lax.axis_size("row")
    iy, iz = lax.axis_index("y"), lax.axis_index("row")
    rows, size = blocks.shape[1:]
    columns = history.shape[2]
    cy = columns // ny
    own = self_inverse.shape[0]
    nlag = ny * nw

    first = blocks[0].reshape(rows, ny, nw, own).transpose(2, 0, 1, 3).reshape(nw, rows, ny * own)
    first = lax.all_to_all(first, W, 0, 0, tiled=True)[0]
    first = lax.all_to_all(first.reshape(ny, rows // ny, ny * own), "y", 0, 0, tiled=True)[0]
    first = exchange(first, "y").reshape(rows, ny * own)

    inverse = exchange(self_inverse, "y").reshape(ny * own, rows)

    before = lax.ppermute(history[1], LAG, [(i, i + 1) for i in range(nlag - 1)])
    field = excitation.transpose(0, 2, 1)
    field = lax.dynamic_slice_in_dim(field, iy * cy, cy, 1)

    part0 = jnp.einsum("lpq,lqc->cp", blocks, history, preferred_element_type=F32)
    part0 = scatter_sum(part0.reshape(ny, cy, rows), "y")
    past1 = jnp.stack([before, history[0]])
    part1 = jnp.einsum("lpq,lqc->cp", blocks, past1, preferred_element_type=F32)
    part1 = scatter_sum(part1.reshape(ny, cy, rows), "y")

    resid0 = field[0] - all_sum(part0, W)
    cur0 = all_sum(times(resid0, inverse, lax.Precision.HIGHEST), "row")
    part1 = part1 + times(cur0.astype(jnp.bfloat16), first)
    resid1 = field[1] - all_sum(part1, W)
    term1 = times(resid1, inverse, lax.Precision.HIGHEST)

    cz = cy // nz
    mine0 = lax.dynamic_slice_in_dim(cur0, iz * cz, cz, 0)
    both = jnp.concatenate([term1, mine0], axis=0)
    both = both.reshape(cy + cz, ny, own).transpose(1, 0, 2).reshape(ny, 1, (cy + cz) * own)
    both = jnp.broadcast_to(both, (ny, nz, (cy + cz) * own)).reshape(ny * nz, (cy + cz) * own)
    got = lax.all_to_all(both, ("y", "row"), 0, 0, tiled=True).reshape(ny, nz, cy + cz, own)
    out1 = jnp.sum(got[:, :, :cy], axis=1).reshape(columns, own)
    out0 = got[:, :, cy:].reshape(columns, own)
    return jnp.stack([out0.T, out1.T])


def solution(mesh):
    n_row = mesh.shape["row"]
    fine = Mesh(np.asarray(mesh.devices).reshape(-1, 4, 2, n_row), ("y", "x", "core", "row"))
    return jax.shard_map(
        shards,
        mesh=fine,
        in_specs=(
            P(LAG, "row", None),
            P(LAG, None, None),
            P(None, "row", None),
            P(LAG, "row"),
        ),
        out_specs=P(None, LAG, None),
        check_vma=False,
    )
```

```python
import numpy as np
import jax
import jax.numpy as jnp
from jax import lax
from jax.sharding import Mesh, PartitionSpec as P

LAG = ("y", "x", "core")
W = ("x", "core")
F32 = jnp.float32
BF16 = jnp.bfloat16


def swap(pieces, axes):
    return lax.all_to_all(pieces, axes, 0, 0, tiled=True)


def everyone(array, axes):
    n = lax.axis_size(axes)
    return jnp.broadcast_to(array, (n, *array.shape))


def split(array):
    high = lax.reduce_precision(array, 8, 7)
    return high.astype(BF16), (array - high).astype(BF16)


def pair_sum(pieces):
    return jnp.sum(pieces.astype(F32), axis=0)


def times(left, right, precision=None):
    return lax.dot_general(
        left, right, (((1,), (1,)), ((), ())), precision=precision, preferred_element_type=F32
    )


def shards(blocks, history, excitation, self_inverse):
    ny, nx, nc, nz = (lax.axis_size(a) for a in ("y", "x", "core", "row"))
    nw = nx * nc
    ix, ic, iw, iz = (lax.axis_index(a) for a in ("x", "core", W, "row"))
    rows, size = blocks.shape[1:]
    columns = history.shape[2]
    cw = columns // nw
    own = self_inverse.shape[0]
    nlag = ny * nw
    cut = rows // nw
    span = nw * own

    whole = blocks[0]
    half = rows // nc
    mine = whole[:half]
    for c in range(1, nc):
        got = lax.ppermute(whole[c * half : (c + 1) * half], LAG, [(0, c)])
        mine = jnp.where(ic == c, got, mine)
    piece = mine[:cut]
    for k in range(1, nx):
        route = [(c, k * nc + c) for c in range(nc)]
        got = lax.ppermute(mine[k * cut : (k + 1) * cut], LAG, route)
        piece = jnp.where(ix == k, got, piece)

    before = lax.ppermute(history[1], LAG, [(i, i + 1) for i in range(nlag - 1)])
    field = excitation.transpose(0, 2, 1)
    field = lax.dynamic_slice_in_dim(field, iw * cw, cw, 1)

    part0 = jnp.einsum("lpq,lqc->cp", blocks, history, preferred_element_type=F32)
    send = jnp.concatenate([part0.reshape(nw, cw, rows), everyone(self_inverse, W)], axis=1)
    got = swap(send, W)
    part0 = jnp.sum(got[:, :cw], axis=0)
    inverse = got[:, cw:].reshape(span, rows)

    pair = everyone(jnp.concatenate(split(part0), axis=0), "y")
    piece = piece.reshape(cut, ny, span).transpose(1, 0, 2)
    got = swap(jnp.concatenate([pair, piece], axis=1), "y")
    resid0 = field[0] - pair_sum(got[:, :cw]) - pair_sum(got[:, cw : 2 * cw])
    piece = got[0, 2 * cw :]

    past1 = jnp.stack([before, history[0]])
    part1 = jnp.einsum("lpq,lqc->cp", blocks, past1, preferred_element_type=F32)
    high, low = split(part1.reshape(nw, cw, rows))
    got = swap(jnp.concatenate([high, low, everyone(piece, W)], axis=1), W)
    part1 = pair_sum(got[:, :cw]) + pair_sum(got[:, cw : 2 * cw])
    first = got[:, 2 * cw :].reshape(nx, nc, cut, span).swapaxes(0, 1).reshape(rows, span)

    term0 = times(resid0, inverse, lax.Precision.HIGHEST)
    cur0 = jnp.sum(swap(everyone(term0, "row"), "row"), axis=0)

    part1 = part1 + times(cur0.astype(BF16), first)
    resid1 = field[1] - jnp.sum(swap(everyone(part1, "y"), "y"), axis=0)
    term1 = times(resid1, inverse, lax.Precision.HIGHEST)

    cz = cw // nz
    mine0 = lax.dynamic_slice_in_dim(cur0, iz * cz, cz, 0)
    both = jnp.concatenate([term1, mine0], axis=0)
    both = both.reshape(cw + cz, nw, own).transpose(1, 0, 2).reshape(nw, 1, (cw + cz) * own)
    both = jnp.broadcast_to(both, (nw, nz, (cw + cz) * own)).reshape(nw * nz, (cw + cz) * own)
    got = swap(both, W + ("row",)).reshape(nw, nz, cw + cz, own)
    out1 = jnp.sum(got[:, :, :cw], axis=1).reshape(columns, own)
    out0 = got[:, :, cw:].reshape(columns, own)
    return jnp.stack([out0.T, out1.T])


def solution(mesh):
    n_row = mesh.shape["row"]
    fine = Mesh(np.asarray(mesh.devices).reshape(-1, 4, 2, n_row), ("y", "x", "core", "row"))
    return jax.shard_map(
        shards,
        mesh=fine,
        in_specs=(
            P(LAG, "row", None),
            P(LAG, None, None),
            P(None, "row", None),
            P(LAG, "row"),
        ),
        out_specs=P(None, LAG, None),
        check_vma=False,
    )
```

```python
import numpy as np
import jax
import jax.numpy as jnp
from jax import lax
from jax.experimental import pallas as pl
from jax.experimental.pallas import tpu as pltpu
from jax.sharding import Mesh, PartitionSpec as P

LAG = ("y", "x", "core")
W = ("x", "core")
F32 = jnp.float32
BF16 = jnp.bfloat16


def swap(pieces, axes):
    return lax.all_to_all(pieces, axes, 0, 0, tiled=True)


def call(body, outs, flops, *args, scratch=()):
    single = not isinstance(outs, list)
    outs = [outs] if single else outs
    shapes = [jax.ShapeDtypeStruct(s, d) for s, d in outs]
    size = sum(a.size * a.dtype.itemsize for a in args)
    size += sum(s.size * s.dtype.itemsize for s in shapes)
    spaces = [pltpu.SMEM if a.dtype == jnp.int32 else pltpu.VMEM for a in args]
    return pl.pallas_call(
        body,
        out_shape=shapes[0] if single else shapes,
        in_specs=[pl.BlockSpec(memory_space=m) for m in spaces],
        scratch_shapes=scratch,
        cost_estimate=pl.CostEstimate(flops=flops, bytes_accessed=size, transcendentals=0),
        compiler_params=pltpu.CompilerParams(vmem_limit_bytes=24 * 1024 * 1024),
    )(*args)


def mm(left, right, precision=None):
    return jnp.dot(left, right, precision=precision, preferred_element_type=F32)


def mm_t(left, right, precision=None):
    return lax.dot_general(
        left, right, (((1,), (1,)), ((), ())), precision=precision, preferred_element_type=F32
    )


def parts(array):
    high = array.astype(BF16)
    return high, (array - high.astype(F32)).astype(BF16)


def sum_first(ref, start, stop):
    total = ref[0, start:stop].astype(F32)
    for i in range(1, ref.shape[0]):
        total = total + ref[i, start:stop].astype(F32)
    return total


def sum_pairs(ref, start, count):
    return sum_first(ref, start, start + count) + sum_first(ref, start + count, start + 2 * count)


def first_sums(where, blocks, history, excitation, inverse, out, field, turned):
    nw = out.shape[0]
    total = mm(blocks[0], history[0]) + mm(blocks[1], history[1])
    total = total.T
    cw = total.shape[0] // nw
    for w in range(nw):
        out[w, :cw] = total[w * cw : (w + 1) * cw]
        out[w, cw:] = inverse[...]
    start = pl.multiple_of(where[1] * cw, cw)
    for s in range(excitation.shape[0]):
        turned[...] = excitation[s].T
        field[s] = turned[pl.ds(start, cw)]


def second_step(where, got, blocks, before, history, got1, got2, got3, out, later):
    ny, depth, span = out.shape
    cut = got1.shape[0]
    cw = (depth - cut) // 2
    high, low = parts(sum_first(got, 0, cw))
    piece = blocks[0, :cut]
    for k, other in enumerate((got1, got2, got3)):
        piece = jnp.where(where[0] == k + 1, other[...], piece)
    for y in range(ny):
        out[y, :cw] = high
        out[y, cw : 2 * cw] = low
        out[y, 2 * cw :] = piece[:, y * span : (y + 1) * span]
    later[...] = (mm(blocks[0], before[...]) + mm(blocks[1], history[0])).T


def third_step(got, later, out):
    nw = out.shape[0]
    cw = later.shape[0] // nw
    for w in range(nw):
        high, low = parts(later[w * cw : (w + 1) * cw])
        out[w, :cw] = high
        out[w, cw : 2 * cw] = low
        out[w, 2 * cw :] = got[0, 2 * cw :]


def fourth_step(got1, got2, got3, field, out, part1, first):
    nz, cw, rows = out.shape
    inverse = got1[:, cw:].reshape(-1, rows)
    resid = field[0] - sum_pairs(got2, 0, cw)
    term = mm_t(resid, inverse, lax.Precision.HIGHEST)
    for z in range(nz):
        out[z] = term
    part1[...] = sum_pairs(got3, 0, cw)
    cut = got3.shape[1] - 2 * cw
    for x in range(first.shape[0] // cut):
        first[x * cut : (x + 1) * cut] = got3[2 * x, 2 * cw :]


def fifth_step(where, got, part1, first, out, mine):
    value = sum_first(got, 0, got.shape[1])
    total = part1[...] + mm_t(value.astype(BF16), first[...])
    for y in range(out.shape[0]):
        out[y] = total
    cz = mine.shape[0]
    share = value[:cz]
    for z in range(1, value.shape[0] // cz):
        share = jnp.where(where[2] == z, value[z * cz : (z + 1) * cz], share)
    mine[...] = share


def sixth_step(got1, got, field, mine, out):
    cw = got.shape[1]
    inverse = got1[:, cw:].reshape(-1, got.shape[2])
    resid = field[1] - sum_first(got, 0, cw)
    out[:cw] = mm_t(resid, inverse, lax.Precision.HIGHEST)
    out[cw:] = mine[...]


def shards(blocks, history, excitation, self_inverse):
    ny, nx, nc, nz = (lax.axis_size(a) for a in ("y", "x", "core", "row"))
    nw = nx * nc
    ix, iw, iz = (lax.axis_index(a) for a in ("x", W, "row"))
    rows, size = blocks.shape[1:]
    columns = history.shape[2]
    cw = columns // nw
    own = self_inverse.shape[0]
    nlag = ny * nw
    cut = rows // nx
    span = nw * own
    work = 2 * rows * size * columns * 2
    small = 2 * cw * rows * span

    where = jnp.stack([ix, iw, iz]).astype(jnp.int32)

    pieces = []
    for k in range(1, nx):
        rows_of_k = blocks[0, k * cut : (k + 1) * cut]
        pieces.append(lax.ppermute(rows_of_k, LAG, [(0, k * nc)]))
    before = lax.ppermute(history[1], LAG, [(i, i + 1) for i in range(nlag - 1)])

    outs = [((nw, cw + own, rows), F32), ((2, cw, rows), F32)]
    turned = [pltpu.VMEM((columns, rows), F32)]
    args = where, blocks, history, excitation, self_inverse
    send, field = call(first_sums, outs, work, *args, scratch=turned)
    got1 = swap(send, W)
    outs = [((ny, 2 * cw + cut, span), BF16), ((columns, rows), F32)]
    args = where, got1, blocks, before, history, *pieces
    send, later = call(second_step, outs, work, *args)
    got2 = swap(send, "y")
    send = call(third_step, ((nw, 2 * cw + cut, rows), BF16), small, got2, later)
    got3 = swap(send, W)
    outs = [((nz, cw, rows), F32), ((cw, rows), F32), ((rows, span), BF16)]
    send, part1, first = call(fourth_step, outs, small, got1, got2, got3, field)
    got4 = swap(send, "row")
    cz = cw // nz
    outs = [((ny, cw, rows), F32), ((cz, span), F32)]
    send, mine0 = call(fifth_step, outs, small, where, got4, part1, first)
    got5 = swap(send, "y")
    both = call(sixth_step, ((cw + cz, span), F32), small, got1, got5, field, mine0)
    both = both.reshape(cw + cz, nw, own).transpose(1, 0, 2).reshape(nw, 1, (cw + cz) * own)
    both = jnp.broadcast_to(both, (nw, nz, (cw + cz) * own)).reshape(nw * nz, (cw + cz) * own)
    got = swap(both, W + ("row",)).reshape(nw, nz, cw + cz, own)
    out1 = jnp.sum(got[:, :, :cw], axis=1).reshape(columns, own)
    out0 = got[:, :, cw:].reshape(columns, own)
    return jnp.stack([out0.T, out1.T])


def solution(mesh):
    n_row = mesh.shape["row"]
    fine = Mesh(np.asarray(mesh.devices).reshape(-1, 4, 2, n_row), ("y", "x", "core", "row"))
    return jax.shard_map(
        shards,
        mesh=fine,
        in_specs=(
            P(LAG, "row", None),
            P(LAG, None, None),
            P(None, "row", None),
            P(LAG, "row"),
        ),
        out_specs=P(None, LAG, None),
        check_vma=False,
    )
```

```python
import numpy as np
import jax
import jax.numpy as jnp
from jax import lax
from jax.experimental import pallas as pl
from jax.experimental.pallas import tpu as pltpu
from jax.sharding import Mesh, PartitionSpec as P

LAG = ("y", "x", "core")
W = ("x", "core")
F32 = jnp.float32
BF16 = jnp.bfloat16


def swap(pieces, axes):
    return lax.all_to_all(pieces, axes, 0, 0, tiled=True)


def call(body, outs, flops, *args, scratch=(), held=None, given=None, limit=24):
    single = not isinstance(outs, list)
    outs = [outs] if single else outs
    shapes = [jax.ShapeDtypeStruct(s, d) for s, d in outs]
    size = sum(a.size * a.dtype.itemsize for a in args)
    size += sum(s.size * s.dtype.itemsize for s in shapes)
    held = held or [pltpu.SMEM if a.dtype == jnp.int32 else pltpu.VMEM for a in args]
    given = given or [pltpu.VMEM] * len(outs)
    specs = [pl.BlockSpec(memory_space=m) for m in given]
    return pl.pallas_call(
        body,
        out_shape=shapes[0] if single else shapes,
        in_specs=[pl.BlockSpec(memory_space=m) for m in held],
        out_specs=specs[0] if single else specs,
        scratch_shapes=scratch,
        cost_estimate=pl.CostEstimate(flops=flops, bytes_accessed=size, transcendentals=0),
        compiler_params=pltpu.CompilerParams(vmem_limit_bytes=limit * 1024 * 1024),
    )(*args)


def mm(left, right, precision=None):
    return jnp.dot(left, right, precision=precision, preferred_element_type=F32)


def mm_t(left, right, precision=None):
    return lax.dot_general(
        left, right, (((1,), (1,)), ((), ())), precision=precision, preferred_element_type=F32
    )


def parts(array):
    high = array.astype(BF16)
    return high, (array - high.astype(F32)).astype(BF16)


def sum_first(ref, start, stop):
    total = ref[0, start:stop].astype(F32)
    for i in range(1, ref.shape[0]):
        total = total + ref[i, start:stop].astype(F32)
    return total


def sum_pairs(ref, start, count):
    return sum_first(ref, start, start + count) + sum_first(ref, start + count, start + 2 * count)


def first_sums(
    where, blocks, history, excitation, inverse, out, field, b, h, e, own, turned, o, f, sems
):
    loads = [
        pltpu.make_async_copy(blocks.at[0], b.at[0], sems.at[0]),
        pltpu.make_async_copy(history.at[0], h.at[0], sems.at[1]),
        pltpu.make_async_copy(blocks.at[1], b.at[1], sems.at[2]),
        pltpu.make_async_copy(history.at[1], h.at[1], sems.at[3]),
        pltpu.make_async_copy(inverse, own, sems.at[4]),
        pltpu.make_async_copy(excitation, e, sems.at[5]),
    ]
    for load in loads:
        load.start()
    nw, depth, _ = out.shape
    cw = depth - own.shape[0]
    loads[0].wait()
    loads[1].wait()
    total = mm(b[0], h[0])
    loads[2].wait()
    loads[3].wait()
    total = (total + mm(b[1], h[1])).T
    loads[4].wait()
    for w in range(nw):
        o[w, :cw] = total[w * cw : (w + 1) * cw]
        o[w, cw:] = own[...]
    store = pltpu.make_async_copy(o, out, sems.at[6])
    store.start()
    loads[5].wait()
    start = pl.multiple_of(where[1] * cw, cw)
    for s in range(e.shape[0]):
        turned[...] = e[s].T
        f[s] = turned[pl.ds(start, cw)]
    other = pltpu.make_async_copy(f, field, sems.at[7])
    other.start()
    store.wait()
    other.wait()


def later_sums(blocks, before, history, out, prior, sem):
    load = pltpu.make_async_copy(before, prior, sem)
    load.start()
    total = mm(blocks[1], history[0])
    load.wait()
    out[...] = (total + mm(blocks[0], prior[...])).T


def second_step(where, got, blocks, got1, got2, got3, out, piece, sem):
    cut = piece.shape[0]
    for k, source in enumerate((blocks.at[0, :cut], got1, got2, got3)):

        @pl.when(where[0] == k)
        def _():
            pltpu.make_async_copy(source, piece, sem).start()

    ny, depth, span = out.shape
    cw = (depth - cut) // 2
    high, low = parts(sum_first(got, 0, cw))
    for y in range(ny):
        out[y, :cw] = high
        out[y, cw : 2 * cw] = low
    pltpu.make_async_copy(got1, piece, sem).wait()
    for y in range(ny):
        out[y, 2 * cw :] = piece[:, y * span : (y + 1) * span]


def third_step(got, later, out):
    nw = out.shape[0]
    cw = later.shape[0] // nw
    for w in range(nw):
        high, low = parts(later[w * cw : (w + 1) * cw])
        out[w, :cw] = high
        out[w, cw : 2 * cw] = low
        out[w, 2 * cw :] = got[0, 2 * cw :]


def fourth_step(got1, got2, got3, field, out, part1, first):
    nz, cw, rows = out.shape
    inverse = got1[:, cw:].reshape(-1, rows)
    resid = field[0] - sum_pairs(got2, 0, cw)
    term = mm_t(resid, inverse, lax.Precision.HIGHEST)
    for z in range(nz):
        out[z] = term
    part1[...] = sum_pairs(got3, 0, cw)
    cut = got3.shape[1] - 2 * cw
    for x in range(first.shape[0] // cut):
        first[x * cut : (x + 1) * cut] = got3[2 * x, 2 * cw :]


def fifth_step(where, got, part1, first, out, mine):
    value = sum_first(got, 0, got.shape[1])
    total = part1[...] + mm_t(value.astype(BF16), first[...])
    for y in range(out.shape[0]):
        out[y] = total
    cz = mine.shape[0]
    share = value[:cz]
    for z in range(1, value.shape[0] // cz):
        share = jnp.where(where[2] == z, value[z * cz : (z + 1) * cz], share)
    mine[...] = share


def sixth_step(got1, got, field, mine, out):
    cw = got.shape[1]
    inverse = got1[:, cw:].reshape(-1, got.shape[2])
    resid = field[1] - sum_first(got, 0, cw)
    out[:cw] = mm_t(resid, inverse, lax.Precision.HIGHEST)
    out[cw:] = mine[...]


def shards(blocks, history, excitation, self_inverse):
    ny, nx, nc, nz = (lax.axis_size(a) for a in ("y", "x", "core", "row"))
    nw = nx * nc
    ix, iw, iz = (lax.axis_index(a) for a in ("x", W, "row"))
    rows, size = blocks.shape[1:]
    columns = history.shape[2]
    cw = columns // nw
    own = self_inverse.shape[0]
    nlag = ny * nw
    cut = rows // nx
    span = nw * own
    work = 2 * rows * size * columns * 2
    small = 2 * cw * rows * span

    where = jnp.stack([ix, iw, iz]).astype(jnp.int32)

    pieces = []
    for k in range(1, nx):
        rows_of_k = blocks[0, k * cut : (k + 1) * cut]
        pieces.append(lax.ppermute(rows_of_k, LAG, [(0, k * nc)]))
    before = lax.ppermute(history[1], LAG, [(i, i + 1) for i in range(nlag - 1)])

    outs = [((nw, cw + own, rows), F32), ((2, cw, rows), F32)]
    scratch = [pltpu.VMEM(a.shape, a.dtype) for a in (blocks, history, excitation, self_inverse)]
    scratch += [pltpu.VMEM((columns, rows), F32)] + [pltpu.VMEM(*o) for o in outs]
    scratch += [pltpu.SemaphoreType.DMA((8,))]
    args = where, blocks, history, excitation, self_inverse
    held = [pltpu.SMEM] + [pltpu.HBM] * 4
    send, field = call(
        first_sums, outs, work, *args, scratch=scratch, held=held, given=[pltpu.HBM] * 2, limit=60
    )
    got1 = swap(send, W)
    later = call(
        later_sums,
        ((columns, rows), F32),
        work,
        blocks,
        before,
        history,
        scratch=[pltpu.VMEM(before.shape, BF16), pltpu.SemaphoreType.DMA(())],
        held=[pltpu.VMEM, pltpu.HBM, pltpu.VMEM],
    )
    got1, later = lax.optimization_barrier((got1, later))
    send = call(
        second_step,
        ((ny, 2 * cw + cut, span), BF16),
        small,
        where,
        got1,
        blocks,
        *pieces,
        scratch=[pltpu.VMEM((cut, size), BF16), pltpu.SemaphoreType.DMA(())],
        held=[pltpu.SMEM, pltpu.VMEM] + [pltpu.HBM] * 4,
    )
    got2 = swap(send, "y")
    send = call(third_step, ((nw, 2 * cw + cut, rows), BF16), small, got2, later)
    got3 = swap(send, W)
    outs = [((nz, cw, rows), F32), ((cw, rows), F32), ((rows, span), BF16)]
    send, part1, first = call(fourth_step, outs, small, got1, got2, got3, field)
    got4 = swap(send, "row")
    cz = cw // nz
    outs = [((ny, cw, rows), F32), ((cz, span), F32)]
    send, mine0 = call(fifth_step, outs, small, where, got4, part1, first)
    got5 = swap(send, "y")
    both = call(sixth_step, ((cw + cz, span), F32), small, got1, got5, field, mine0)
    both = both.reshape(cw + cz, nw, own).transpose(1, 0, 2).reshape(nw, 1, (cw + cz) * own)
    both = jnp.broadcast_to(both, (nw, nz, (cw + cz) * own)).reshape(nw * nz, (cw + cz) * own)
    got = swap(both, W + ("row",)).reshape(nw, nz, cw + cz, own)
    out1 = jnp.sum(got[:, :, :cw], axis=1).reshape(columns, own)
    out0 = got[:, :, cw:].reshape(columns, own)
    return jnp.stack([out0.T, out1.T])


def solution(mesh):
    n_row = mesh.shape["row"]
    fine = Mesh(np.asarray(mesh.devices).reshape(-1, 4, 2, n_row), ("y", "x", "core", "row"))
    return jax.shard_map(
        shards,
        mesh=fine,
        in_specs=(
            P(LAG, "row", None),
            P(LAG, None, None),
            P(None, "row", None),
            P(LAG, "row"),
        ),
        out_specs=P(None, LAG, None),
        check_vma=False,
    )
```

```python
import numpy as np
import jax
import jax.numpy as jnp
from jax import lax
from jax.experimental import pallas as pl
from jax.experimental.pallas import tpu as pltpu
from jax.sharding import Mesh, PartitionSpec as P

LAG = ("y", "x", "core")
W = ("x", "core")
F32 = jnp.float32
BF16 = jnp.bfloat16


def swap(pieces, axes):
    return lax.all_to_all(pieces, axes, 0, 0, tiled=True)


def call(body, outs, flops, *args, scratch=(), held=None, given=None, limit=24):
    single = not isinstance(outs, list)
    outs = [outs] if single else outs
    shapes = [jax.ShapeDtypeStruct(s, d) for s, d in outs]
    size = sum(a.size * a.dtype.itemsize for a in args)
    size += sum(s.size * s.dtype.itemsize for s in shapes)
    held = held or [pltpu.SMEM if a.dtype == jnp.int32 else pltpu.VMEM for a in args]
    given = given or [pltpu.VMEM] * len(outs)
    specs = [pl.BlockSpec(memory_space=m) for m in given]
    return pl.pallas_call(
        body,
        out_shape=shapes[0] if single else shapes,
        in_specs=[pl.BlockSpec(memory_space=m) for m in held],
        out_specs=specs[0] if single else specs,
        scratch_shapes=scratch,
        cost_estimate=pl.CostEstimate(flops=flops, bytes_accessed=size, transcendentals=0),
        compiler_params=pltpu.CompilerParams(vmem_limit_bytes=limit * 1024 * 1024),
    )(*args)


def mm(left, right, precision=None):
    return jnp.dot(left, right, precision=precision, preferred_element_type=F32)


def mm_t(left, right, precision=None):
    return lax.dot_general(
        left, right, (((1,), (1,)), ((), ())), precision=precision, preferred_element_type=F32
    )


def parts(array):
    high = array.astype(BF16)
    return high, (array - high.astype(F32)).astype(BF16)


def sum_first(ref, start, stop):
    total = ref[0, start:stop].astype(F32)
    for i in range(1, ref.shape[0]):
        total = total + ref[i, start:stop].astype(F32)
    return total


def sum_pairs(ref, start, count):
    return sum_first(ref, start, start + count) + sum_first(ref, start + count, start + 2 * count)


def first_sums(where, blocks, history, excitation, inverse, out, field, *rest):
    pieces, (b, h, e, own, turned, o, f, sems) = rest[:-8], rest[-8:]
    cut = pieces[0].shape[0]
    loads = [
        pltpu.make_async_copy(blocks.at[0], b.at[0], sems.at[0]),
        pltpu.make_async_copy(history.at[0], h.at[0], sems.at[1]),
        pltpu.make_async_copy(blocks.at[1], b.at[1], sems.at[2]),
        pltpu.make_async_copy(history.at[1], h.at[1], sems.at[3]),
        pltpu.make_async_copy(inverse, own, sems.at[4]),
        pltpu.make_async_copy(excitation, e, sems.at[5]),
    ]
    for load in loads:
        load.start()
    nw, depth, _ = out.shape
    cw = depth - own.shape[0]
    loads[0].wait()
    stores = []
    for k, piece in enumerate(pieces):
        rows = b.at[0, k * cut : (k + 1) * cut]
        stores.append(pltpu.make_async_copy(rows, piece, sems.at[8 + k]))
        stores[-1].start()
    loads[1].wait()
    total = mm(b[0], h[0])
    loads[2].wait()
    loads[3].wait()
    total = (total + mm(b[1], h[1])).T
    loads[4].wait()
    for w in range(nw):
        o[w, :cw] = total[w * cw : (w + 1) * cw]
        o[w, cw:] = own[...]
    stores.append(pltpu.make_async_copy(o, out, sems.at[6]))
    stores[-1].start()
    loads[5].wait()
    start = pl.multiple_of(where[1] * cw, cw)
    for s in range(e.shape[0]):
        turned[...] = e[s].T
        f[s] = turned[pl.ds(start, cw)]
    stores.append(pltpu.make_async_copy(f, field, sems.at[7]))
    stores[-1].start()
    for store in stores:
        store.wait()


def later_sums(blocks, before, history, out, b, h, o, sems):
    loads = [
        pltpu.make_async_copy(blocks.at[1], b.at[1], sems.at[0]),
        pltpu.make_async_copy(history.at[0], h.at[0], sems.at[1]),
        pltpu.make_async_copy(blocks.at[0], b.at[0], sems.at[2]),
        pltpu.make_async_copy(before, h.at[1], sems.at[3]),
    ]
    for load in loads:
        load.start()
    loads[0].wait()
    loads[1].wait()
    total = mm(b[1], h[0])
    loads[2].wait()
    loads[3].wait()
    o[...] = (total + mm(b[0], h[1])).T
    store = pltpu.make_async_copy(o, out, sems.at[0])
    store.start()
    store.wait()


def second_step(where, got, *rest):
    sources, (out, piece, sem) = rest[:-3], rest[-3:]
    cut = piece.shape[0]
    for k, source in enumerate(sources):

        @pl.when(where[0] == k)
        def _():
            pltpu.make_async_copy(source, piece, sem).start()

    ny, depth, span = out.shape
    cw = (depth - cut) // 2
    high, low = parts(sum_first(got, 0, cw))
    for y in range(ny):
        out[y, :cw] = high
        out[y, cw : 2 * cw] = low
    pltpu.make_async_copy(sources[0], piece, sem).wait()
    for y in range(ny):
        out[y, 2 * cw :] = piece[:, y * span : (y + 1) * span]


def third_step(got, later, out):
    nw = out.shape[0]
    cw = later.shape[0] // nw
    for w in range(nw):
        high, low = parts(later[w * cw : (w + 1) * cw])
        out[w, :cw] = high
        out[w, cw : 2 * cw] = low
        out[w, 2 * cw :] = got[0, 2 * cw :]


def fourth_step(got1, got2, got3, field, out, part1, first):
    nz, cw, rows = out.shape
    inverse = got1[:, cw:].reshape(-1, rows)
    resid = field[0] - sum_pairs(got2, 0, cw)
    term = mm_t(resid, inverse, lax.Precision.HIGHEST)
    for z in range(nz):
        out[z] = term
    part1[...] = sum_pairs(got3, 0, cw)
    cut = got3.shape[1] - 2 * cw
    for x in range(first.shape[0] // cut):
        first[x * cut : (x + 1) * cut] = got3[2 * x, 2 * cw :]


def fifth_step(where, got, part1, first, out, mine):
    value = sum_first(got, 0, got.shape[1])
    total = part1[...] + mm_t(value.astype(BF16), first[...])
    for y in range(out.shape[0]):
        out[y] = total
    cz = mine.shape[0]
    share = value[:cz]
    for z in range(1, value.shape[0] // cz):
        share = jnp.where(where[2] == z, value[z * cz : (z + 1) * cz], share)
    mine[...] = share


def sixth_step(got1, got, field, mine, out):
    cw = got.shape[1]
    inverse = got1[:, cw:].reshape(-1, got.shape[2])
    resid = field[1] - sum_first(got, 0, cw)
    out[:cw] = mm_t(resid, inverse, lax.Precision.HIGHEST)
    out[cw:] = mine[...]


def shards(blocks, history, excitation, self_inverse):
    ny, nx, nc, nz = (lax.axis_size(a) for a in ("y", "x", "core", "row"))
    nw = nx * nc
    ix, iw, iz = (lax.axis_index(a) for a in ("x", W, "row"))
    rows, size = blocks.shape[1:]
    columns = history.shape[2]
    cw = columns // nw
    own = self_inverse.shape[0]
    nlag = ny * nw
    cut = rows // nx
    span = nw * own
    work = 2 * rows * size * columns * 2
    small = 2 * cw * rows * span

    where = jnp.stack([ix, iw, iz]).astype(jnp.int32)

    before = lax.ppermute(history[1], LAG, [(i, i + 1) for i in range(nlag - 1)])

    outs = [((nw, cw + own, rows), F32), ((2, cw, rows), F32)] + [((cut, size), BF16)] * nx
    scratch = [pltpu.VMEM(a.shape, a.dtype) for a in (blocks, history, excitation, self_inverse)]
    scratch += [pltpu.VMEM((columns, rows), F32)] + [pltpu.VMEM(*o) for o in outs[:2]]
    scratch += [pltpu.SemaphoreType.DMA((8 + nx,))]
    args = where, blocks, history, excitation, self_inverse
    held = [pltpu.SMEM] + [pltpu.HBM] * 4
    given = [pltpu.HBM] * len(outs)
    send, field, *pieces = call(
        first_sums, outs, work, *args, scratch=scratch, held=held, given=given, limit=60
    )
    got1 = swap(send, W)
    for k in range(1, nx):
        route = [(x * nc, (x + k) % nx * nc) for x in range(nx)]
        pieces[k] = lax.ppermute(pieces[k], LAG, route)
    send = call(
        second_step,
        ((ny, 2 * cw + cut, span), BF16),
        small,
        where,
        got1,
        *pieces,
        scratch=[pltpu.VMEM((cut, size), BF16), pltpu.SemaphoreType.DMA(())],
        held=[pltpu.SMEM, pltpu.VMEM] + [pltpu.HBM] * nx,
    )
    got2 = swap(send, "y")
    later = call(
        later_sums,
        ((columns, rows), F32),
        work,
        blocks,
        before,
        history,
        scratch=[
            pltpu.VMEM(blocks.shape, BF16),
            pltpu.VMEM(history.shape, BF16),
            pltpu.VMEM((columns, rows), F32),
            pltpu.SemaphoreType.DMA((4,)),
        ],
        held=[pltpu.HBM] * 3,
        given=[pltpu.HBM],
        limit=60,
    )
    send = call(third_step, ((nw, 2 * cw + cut, rows), BF16), small, got2, later)
    got3 = swap(send, W)
    outs = [((nz, cw, rows), F32), ((cw, rows), F32), ((rows, span), BF16)]
    send, part1, first = call(fourth_step, outs, small, got1, got2, got3, field)
    got4 = swap(send, "row")
    cz = cw // nz
    outs = [((ny, cw, rows), F32), ((cz, span), F32)]
    send, mine0 = call(fifth_step, outs, small, where, got4, part1, first)
    got5 = swap(send, "y")
    both = call(sixth_step, ((cw + cz, span), F32), small, got1, got5, field, mine0)
    both = both.reshape(cw + cz, nw, own).transpose(1, 0, 2).reshape(nw, 1, (cw + cz) * own)
    both = jnp.broadcast_to(both, (nw, nz, (cw + cz) * own)).reshape(nw * nz, (cw + cz) * own)
    got = swap(both, W + ("row",)).reshape(nw, nz, cw + cz, own)
    out1 = jnp.sum(got[:, :, :cw], axis=1).reshape(columns, own)
    out0 = got[:, :, cw:].reshape(columns, own)
    return jnp.stack([out0.T, out1.T])


def solution(mesh):
    n_row = mesh.shape["row"]
    fine = Mesh(np.asarray(mesh.devices).reshape(-1, 4, 2, n_row), ("y", "x", "core", "row"))
    return jax.shard_map(
        shards,
        mesh=fine,
        in_specs=(
            P(LAG, "row", None),
            P(LAG, None, None),
            P(None, "row", None),
            P(LAG, "row"),
        ),
        out_specs=P(None, LAG, None),
        check_vma=False,
    )
```

```python
import numpy as np
import jax
import jax.numpy as jnp
from jax import lax
from jax.experimental import pallas as pl
from jax.experimental.pallas import tpu as pltpu
from jax.sharding import Mesh, PartitionSpec as P

LAG = ("y", "x", "core")
W = ("x", "core")
F32 = jnp.float32
BF16 = jnp.bfloat16


def swap(pieces, axes):
    return lax.all_to_all(pieces, axes, 0, 0, tiled=True)


def call(body, outs, flops, *args, scratch=(), held=None, given=None, limit=24):
    single = not isinstance(outs, list)
    outs = [outs] if single else outs
    shapes = [jax.ShapeDtypeStruct(s, d) for s, d in outs]
    size = sum(a.size * a.dtype.itemsize for a in args)
    size += sum(s.size * s.dtype.itemsize for s in shapes)
    held = held or [pltpu.VMEM] * len(args)
    given = given or [pltpu.VMEM] * len(outs)
    specs = [pl.BlockSpec(memory_space=m) for m in given]
    return pl.pallas_call(
        body,
        out_shape=shapes[0] if single else shapes,
        in_specs=[pl.BlockSpec(memory_space=m) for m in held],
        out_specs=specs[0] if single else specs,
        scratch_shapes=scratch,
        cost_estimate=pl.CostEstimate(flops=flops, bytes_accessed=size, transcendentals=0),
        compiler_params=pltpu.CompilerParams(vmem_limit_bytes=limit * 1024 * 1024),
    )(*args)


def mm(left, right, precision=None):
    return jnp.dot(left, right, precision=precision, preferred_element_type=F32)


def mm_t(left, right, precision=None):
    return lax.dot_general(
        left, right, (((1,), (1,)), ((), ())), precision=precision, preferred_element_type=F32
    )


def parts(array):
    high = array.astype(BF16)
    return high, (array - high.astype(F32)).astype(BF16)


def sum_first(ref, start, stop):
    total = ref[0, start:stop].astype(F32)
    for i in range(1, ref.shape[0]):
        total = total + ref[i, start:stop].astype(F32)
    return total


def first_sums(blocks, history, excitation, inverse, out, field, *rest):
    pieces, (b, h, e, own, turned, slabs, o, f, sems) = rest[:-9], rest[-9:]
    loads = [
        pltpu.make_async_copy(history.at[0], h.at[0], sems.at[0]),
        pltpu.make_async_copy(blocks.at[0], b.at[0], sems.at[1]),
        pltpu.make_async_copy(history.at[1], h.at[1], sems.at[2]),
        pltpu.make_async_copy(blocks.at[1], b.at[1], sems.at[3]),
        pltpu.make_async_copy(inverse, own, sems.at[4]),
        pltpu.make_async_copy(excitation, e, sems.at[5]),
    ]
    for load in loads:
        load.start()
    nw, depth, rows = out.shape
    cw = depth - own.shape[0]
    loads[0].wait()
    loads[1].wait()
    total = mm(b[0], h[0])
    loads[2].wait()
    loads[3].wait()
    total = (total + mm(b[1], h[1])).T
    loads[4].wait()
    for w in range(nw):
        o[w, :cw] = total[w * cw : (w + 1) * cw]
        o[w, cw:] = own[...]
    store = pltpu.make_async_copy(o, out, sems.at[6])
    store.start()
    loads[5].wait()
    start = pl.multiple_of(lax.axis_index(W) * cw, cw)
    for s in range(e.shape[0]):
        turned[...] = e[s].T
        f[s] = turned[pl.ds(start, cw)]
    other = pltpu.make_async_copy(f, field, sems.at[7])
    other.start()

    @pl.when(lax.axis_index(LAG) == 0)
    def _():
        nx = len(pieces)
        span = nw * own.shape[0]
        cut = span // nx
        for y in range(b.shape[2] // span):
            slab = b[0, :, y * span : (y + 1) * span].T
            for x in range(nx):
                slabs[x, y * cut : (y + 1) * cut] = slab[x * cut : (x + 1) * cut]
        stores = []
        for x in range(nx):
            stores.append(pltpu.make_async_copy(slabs.at[x], pieces[x], sems.at[8 + x]))
            stores[-1].start()
        for s in stores:
            s.wait()

    store.wait()
    other.wait()


def later_sums(blocks, before, history, out):
    out[...] = (mm(blocks[1], history[0]) + mm(blocks[0], before[...])).T


def second_step(got, *rest):
    sources, (out, piece, sem) = rest[:-3], rest[-3:]
    for k, source in enumerate(sources):

        @pl.when(lax.axis_index("x") == k)
        def _():
            pltpu.make_async_copy(source, piece, sem).start()

    peers, depth, _ = out.shape
    cut = piece.shape[0] // peers
    cw = (depth - cut) // 2
    high, low = parts(sum_first(got, 0, cw))
    for i in range(peers):
        out[i, :cw] = high
        out[i, cw : 2 * cw] = low
    pltpu.make_async_copy(sources[0], piece, sem).wait()
    for i in range(peers):
        out[i, 2 * cw :] = piece[i * cut : (i + 1) * cut]


def third_step(got1, got2, field, out):
    cw = out.shape[0]
    inverse = got1[:, cw:].reshape(-1, out.shape[1])
    core = lax.axis_index("core")
    total = field[0]
    for y in range(got2.shape[0] // 2):
        pair = got2[2 * y + core, : 2 * cw].astype(F32)
        total = total - (pair[:cw] + pair[cw:])
    out[...] = mm_t(total, inverse, lax.Precision.HIGHEST)


def fourth_step(current, got2, later, out):
    nw, cw, _ = out.shape
    first = got2[0, 2 * cw :]
    total = later[...] + mm(current[...].astype(BF16), first)
    for w in range(nw):
        out[w] = total[w * cw : (w + 1) * cw]


def fifth_step(got, out):
    total = sum_first(got, 0, got.shape[1])
    for y in range(out.shape[0]):
        out[y] = total


def sixth_step(got1, got, field, out):
    cw = got.shape[1]
    inverse = got1[:, cw:].reshape(-1, got.shape[2])
    resid = field[1] - sum_first(got, 0, cw)
    out[...] = mm_t(resid, inverse, lax.Precision.HIGHEST)


def to_owners(terms, nw, nz):
    cw, span = terms.shape
    own = span // nw
    sends = terms.reshape(cw, nw, own).transpose(1, 0, 2).reshape(nw, 1, cw * own)
    sends = jnp.broadcast_to(sends, (nw, nz, cw * own)).reshape(nw * nz, cw * own)
    got = swap(sends, W + ("row",)).reshape(nw, nz, cw, own)
    return jnp.sum(got, axis=1).reshape(nw * cw, own)


def shards(blocks, history, excitation, self_inverse):
    ny, nx, nc, nz = (lax.axis_size(a) for a in ("y", "x", "core", "row"))
    nw = nx * nc
    rows, size = blocks.shape[1:]
    columns = history.shape[2]
    cw = columns // nw
    own = self_inverse.shape[0]
    nlag = ny * nw
    span = nw * own
    work = 2 * rows * size * columns * 2
    small = 2 * cw * rows * span

    before = lax.ppermute(history[1], LAG, [(i, i + 1) for i in range(nlag - 1)])
    later = call(later_sums, ((columns, rows), F32), work, blocks, before, history)

    part = (ny * nc * own, rows)
    outs = [((nw, cw + own, rows), F32), ((2, cw, rows), F32)] + [(part, BF16)] * nx
    scratch = [pltpu.VMEM(a.shape, a.dtype) for a in (blocks, history, excitation, self_inverse)]
    scratch += [pltpu.VMEM((columns, rows), F32), pltpu.VMEM((nx, *part), BF16)]
    scratch += [pltpu.VMEM(*o) for o in outs[:2]] + [pltpu.SemaphoreType.DMA((8 + nx,))]
    args = blocks, history, excitation, self_inverse
    held, given = [pltpu.HBM] * len(args), [pltpu.HBM] * len(outs)
    send, field, *pieces = call(
        first_sums, outs, work, *args, scratch=scratch, held=held, given=given, limit=60
    )
    got1 = swap(send, W)
    for k in range(1, nx):
        pieces[k] = lax.ppermute(pieces[k], LAG, [(0, k * nc)])
    got1, later = lax.optimization_barrier((got1, later))
    send = call(
        second_step,
        ((ny * nc, 2 * cw + own, rows), BF16),
        small,
        got1,
        *pieces,
        scratch=[pltpu.VMEM(part, BF16), pltpu.SemaphoreType.DMA(())],
        held=[pltpu.VMEM] + [pltpu.HBM] * nx,
    )
    got2 = swap(send, ("y", "core"))
    term = call(third_step, ((cw, span), F32), small, got1, got2, field)
    current0 = to_owners(term, nw, nz)
    send = call(fourth_step, ((nw, cw, rows), F32), small, current0, got2, later)
    got4 = swap(send, W)
    send = call(fifth_step, ((ny, cw, rows), F32), small, got4)
    got5 = swap(send, "y")
    term = call(sixth_step, ((cw, span), F32), small, got1, got5, field)
    current1 = to_owners(term, nw, nz)
    current0, current1 = lax.optimization_barrier((current0, current1))
    return jnp.stack([current0.T, current1.T])


def solution(mesh):
    n_row = mesh.shape["row"]
    fine = Mesh(np.asarray(mesh.devices).reshape(-1, 4, 2, n_row), ("y", "x", "core", "row"))
    return jax.shard_map(
        shards,
        mesh=fine,
        in_specs=(
            P(LAG, "row", None),
            P(LAG, None, None),
            P(None, "row", None),
            P(LAG, "row"),
        ),
        out_specs=P(None, LAG, None),
        check_vma=False,
    )
```

```python
import numpy as np
import jax
import jax.numpy as jnp
from jax import lax
from jax.experimental import pallas as pl
from jax.experimental.pallas import tpu as pltpu
from jax.sharding import Mesh, PartitionSpec as P

LAG = ("y", "x", "core")
W = ("x", "core")
F32 = jnp.float32
BF16 = jnp.bfloat16


def swap(pieces, axes):
    return lax.all_to_all(pieces, axes, 0, 0, tiled=True)


def call(body, outs, flops, *args, scratch=(), held=None, given=None, limit=24):
    single = not isinstance(outs, list)
    outs = [outs] if single else outs
    shapes = [jax.ShapeDtypeStruct(s, d) for s, d in outs]
    size = sum(a.size * a.dtype.itemsize for a in args)
    size += sum(s.size * s.dtype.itemsize for s in shapes)
    held = held or [pltpu.VMEM] * len(args)
    given = given or [pltpu.VMEM] * len(outs)
    specs = [pl.BlockSpec(memory_space=m) for m in given]
    return pl.pallas_call(
        body,
        out_shape=shapes[0] if single else shapes,
        in_specs=[pl.BlockSpec(memory_space=m) for m in held],
        out_specs=specs[0] if single else specs,
        scratch_shapes=scratch,
        cost_estimate=pl.CostEstimate(flops=flops, bytes_accessed=size, transcendentals=0),
        compiler_params=pltpu.CompilerParams(vmem_limit_bytes=limit * 1024 * 1024),
    )(*args)


def mm(left, right, precision=None):
    return jnp.dot(left, right, precision=precision, preferred_element_type=F32)


def mm_t(left, right, precision=None):
    return lax.dot_general(
        left, right, (((1,), (1,)), ((), ())), precision=precision, preferred_element_type=F32
    )


def parts(array):
    high = array.astype(BF16)
    return high, (array - high.astype(F32)).astype(BF16)


def sum_first(ref, start, stop):
    total = ref[0, start:stop].astype(F32)
    for i in range(1, ref.shape[0]):
        total = total + ref[i, start:stop].astype(F32)
    return total


def sum_pairs(ref, start, count):
    return sum_first(ref, start, start + count) + sum_first(ref, start + count, start + 2 * count)


def less_field(total, field):
    return jnp.where(lax.axis_index(LAG) == 0, total - field, total).T


def last_of(history, out, sems):
    count = sems.shape[0]
    step = out.shape[0] // count
    loads = []
    for i in range(count):
        rows = pl.ds(i * step, step)
        loads.append(pltpu.make_async_copy(history.at[1, rows], out.at[rows], sems.at[i]))
        loads[-1].start()
    for load in loads:
        load.wait()


def first_sums(blocks, history, excitation, inverse, out, lead, *rest):
    pieces, (b, h, e, own, o, f, sems) = rest[:-7], rest[-7:]
    cut = pieces[0].shape[0]
    loads = [
        pltpu.make_async_copy(history.at[0], h.at[0], sems.at[0]),
        pltpu.make_async_copy(blocks.at[0], b.at[0], sems.at[1]),
        pltpu.make_async_copy(history.at[1], h.at[1], sems.at[2]),
        pltpu.make_async_copy(blocks.at[1], b.at[1], sems.at[3]),
        pltpu.make_async_copy(inverse, own, sems.at[4]),
        pltpu.make_async_copy(excitation, e, sems.at[5]),
    ]
    for load in loads:
        load.start()
    nw, depth, _ = out.shape
    cw = depth - own.shape[0]
    loads[0].wait()
    loads[1].wait()
    stores = []
    for k, piece in enumerate(pieces):
        rows = b.at[0, (k + 1) * cut : (k + 2) * cut]
        stores.append(pltpu.make_async_copy(rows, piece, sems.at[8 + k]))
        stores[-1].start()
    total = mm(b[0], h[0])
    loads[2].wait()
    loads[3].wait()
    total = total + mm(b[1], h[1])
    loads[4].wait()
    loads[5].wait()
    total = less_field(total, e[0])
    for w in range(nw):
        o[w, :cw] = total[w * cw : (w + 1) * cw]
        o[w, cw:] = own[...]
    stores.append(pltpu.make_async_copy(o, out, sems.at[6]))
    stores[-1].start()
    f[...] = less_field(jnp.zeros_like(e[1]), e[1])
    stores.append(pltpu.make_async_copy(f, lead, sems.at[7]))
    stores[-1].start()
    for store in stores:
        store.wait()


def later_sums(blocks, before, history, out):
    out[...] = (mm(blocks[1], history[0]) + mm(blocks[0], before[...])).T


def second_step(got, blocks, *rest):
    sources, (out, piece, sem) = rest[:-3], rest[-3:]
    sources = (blocks.at[0, : piece.shape[0]], *sources)
    for k, source in enumerate(sources):

        @pl.when(lax.axis_index("x") == k)
        def _():
            pltpu.make_async_copy(source, piece, sem).start()

    ny, depth, span = out.shape
    cw = (depth - piece.shape[0]) // 2
    high, low = parts(sum_first(got, 0, cw))
    for y in range(ny):
        out[y, :cw] = high
        out[y, cw : 2 * cw] = low
    pltpu.make_async_copy(sources[0], piece, sem).wait()
    for y in range(ny):
        out[y, 2 * cw :] = piece[:, y * span : (y + 1) * span]


def third_step(got, later, lead, out):
    nw = out.shape[0]
    cw = later.shape[0] // nw
    total = later[...] + lead[...]
    for w in range(nw):
        high, low = parts(total[w * cw : (w + 1) * cw])
        out[w, :cw] = high
        out[w, cw : 2 * cw] = low
        out[w, 2 * cw :] = got[0, 2 * cw :]


def fourth_step(got1, got2, got3, out, part1, first):
    nz, cw, rows = out.shape
    inverse = got1[:, cw:].reshape(-1, rows)
    term = -mm_t(sum_pairs(got2, 0, cw), inverse, lax.Precision.HIGHEST)
    for z in range(nz):
        out[z] = term
    part1[...] = sum_pairs(got3, 0, cw)
    cut = got3.shape[1] - 2 * cw
    for x in range(first.shape[0] // cut):
        first[x * cut : (x + 1) * cut] = got3[2 * x, 2 * cw :]


def fifth_step(got, part1, first, out, mine):
    value = sum_first(got, 0, got.shape[1])
    total = part1[...] + mm_t(value.astype(BF16), first[...])
    for y in range(out.shape[0]):
        out[y] = total
    cz = mine.shape[0]
    share = value[:cz]
    for z in range(1, value.shape[0] // cz):
        share = jnp.where(lax.axis_index("row") == z, value[z * cz : (z + 1) * cz], share)
    mine[...] = share


def sixth_step(got1, got, mine, out):
    cw = got.shape[1]
    inverse = got1[:, cw:].reshape(-1, got.shape[2])
    out[:cw] = -mm_t(sum_first(got, 0, cw), inverse, lax.Precision.HIGHEST)
    out[cw:] = mine[...]


def shards(blocks, history, excitation, self_inverse):
    ny, nx, nc, nz = (lax.axis_size(a) for a in ("y", "x", "core", "row"))
    nw = nx * nc
    rows, size = blocks.shape[1:]
    columns = history.shape[2]
    cw = columns // nw
    own = self_inverse.shape[0]
    nlag = ny * nw
    cut = rows // nx
    span = nw * own
    work = 2 * rows * size * columns * 2
    small = 2 * cw * rows * span

    before = call(
        last_of,
        (history.shape[1:], BF16),
        0,
        history,
        scratch=[pltpu.SemaphoreType.DMA((4,))],
        held=[pltpu.HBM],
        given=[pltpu.HBM],
        limit=60,
    )
    before = lax.ppermute(before, LAG, [(i, i + 1) for i in range(nlag - 1)])
    later = call(later_sums, ((columns, rows), F32), work, blocks, before, history)

    outs = [((nw, cw + own, rows), F32), ((columns, rows), F32)] + [((cut, size), BF16)] * (nx - 1)
    scratch = [pltpu.VMEM(blocks.shape, BF16), pltpu.VMEM(history.shape, BF16)]
    scratch += [pltpu.VMEM(excitation.shape, F32), pltpu.VMEM((own, rows), F32)]
    scratch += [pltpu.VMEM(*o) for o in outs[:2]] + [pltpu.SemaphoreType.DMA((8 + nx,))]
    args = blocks, history, excitation, self_inverse
    held, given = [pltpu.HBM] * len(args), [pltpu.HBM] * len(outs)
    send, lead, *pieces = call(
        first_sums, outs, work, *args, scratch=scratch, held=held, given=given, limit=60
    )
    got1 = swap(send, W)
    for k in range(1, nx):
        pieces[k - 1] = lax.ppermute(pieces[k - 1], LAG, [(0, k * nc)])
    got1, later = lax.optimization_barrier((got1, later))
    send = call(
        second_step,
        ((ny, 2 * cw + cut, span), BF16),
        small,
        got1,
        blocks,
        *pieces,
        scratch=[pltpu.VMEM((cut, size), BF16), pltpu.SemaphoreType.DMA(())],
        held=[pltpu.VMEM] + [pltpu.HBM] * nx,
    )
    got2 = swap(send, "y")
    send = call(third_step, ((nw, 2 * cw + cut, rows), BF16), small, got2, later, lead)
    got3 = swap(send, W)
    outs = [((nz, cw, rows), F32), ((cw, rows), F32), ((rows, span), BF16)]
    send, part1, first = call(fourth_step, outs, small, got1, got2, got3)
    got4 = swap(send, "row")
    cz = cw // nz
    outs = [((ny, cw, rows), F32), ((cz, span), F32)]
    send, mine0 = call(fifth_step, outs, small, got4, part1, first)
    got5 = swap(send, "y")
    both = call(sixth_step, ((cw + cz, span), F32), small, got1, got5, mine0)
    both = both.reshape(cw + cz, nw, own).transpose(1, 0, 2).reshape(nw, 1, (cw + cz) * own)
    both = jnp.broadcast_to(both, (nw, nz, (cw + cz) * own)).reshape(nw * nz, (cw + cz) * own)
    got = swap(both, W + ("row",)).reshape(nw, nz, cw + cz, own)
    out1 = jnp.sum(got[:, :, :cw], axis=1).reshape(columns, own)
    out0 = got[:, :, cw:].reshape(columns, own)
    return jnp.stack([out0.T, out1.T])


def solution(mesh):
    n_row = mesh.shape["row"]
    fine = Mesh(np.asarray(mesh.devices).reshape(-1, 4, 2, n_row), ("y", "x", "core", "row"))
    return jax.shard_map(
        shards,
        mesh=fine,
        in_specs=(
            P(LAG, "row", None),
            P(LAG, None, None),
            P(None, "row", None),
            P(LAG, "row"),
        ),
        out_specs=P(None, LAG, None),
        check_vma=False,
    )
```

```python
import numpy as np
import jax
import jax.numpy as jnp
from jax import lax
from jax.experimental import pallas as pl
from jax.experimental.pallas import tpu as pltpu
from jax.sharding import Mesh, PartitionSpec as P

LAG = ("y", "x", "core")
W = ("x", "core")
ORDER = (2, 3, 1)
F32 = jnp.float32
BF16 = jnp.bfloat16


def swap(pieces, axes):
    return lax.all_to_all(pieces, axes, 0, 0, tiled=True)


def call(body, outs, flops, *args, scratch=(), held=None, given=None, limit=24):
    single = not isinstance(outs, list)
    outs = [outs] if single else outs
    shapes = [jax.ShapeDtypeStruct(s, d) for s, d in outs]
    size = sum(a.size * a.dtype.itemsize for a in args)
    size += sum(s.size * s.dtype.itemsize for s in shapes)
    held = held or [pltpu.VMEM] * len(args)
    given = given or [pltpu.VMEM] * len(outs)
    specs = [pl.BlockSpec(memory_space=m) for m in given]
    return pl.pallas_call(
        body,
        out_shape=shapes[0] if single else shapes,
        in_specs=[pl.BlockSpec(memory_space=m) for m in held],
        out_specs=specs[0] if single else specs,
        scratch_shapes=scratch,
        cost_estimate=pl.CostEstimate(flops=flops, bytes_accessed=size, transcendentals=0),
        compiler_params=pltpu.CompilerParams(vmem_limit_bytes=limit * 1024 * 1024),
    )(*args)


def mm(left, right, precision=None):
    return jnp.dot(left, right, precision=precision, preferred_element_type=F32)


def mm_t(left, right, precision=None):
    return lax.dot_general(
        left, right, (((1,), (1,)), ((), ())), precision=precision, preferred_element_type=F32
    )


def parts(array):
    high = array.astype(BF16)
    return high, (array - high.astype(F32)).astype(BF16)


def sum_first(ref, start, stop):
    total = ref[0, start:stop].astype(F32)
    for i in range(1, ref.shape[0]):
        total = total + ref[i, start:stop].astype(F32)
    return total


def sum_pairs(ref, start, count):
    return sum_first(ref, start, start + count) + sum_first(ref, start + count, start + 2 * count)


def less_field(total, field):
    return jnp.where(lax.axis_index(LAG) == 0, total - field, total).T


def last_of(history, out, sems):
    count = sems.shape[0]
    step = out.shape[0] // count
    loads = []
    for i in range(count):
        rows = pl.ds(i * step, step)
        loads.append(pltpu.make_async_copy(history.at[1, rows], out.at[rows], sems.at[i]))
        loads[-1].start()
    for load in loads:
        load.wait()


def first_sums(blocks, history, excitation, inverse, out, lead, *rest):
    pieces, (b, h, e, own, o, f, sems) = rest[:-7], rest[-7:]
    cut = pieces[0].shape[0]
    loads = [
        pltpu.make_async_copy(history.at[0], h.at[0], sems.at[0]),
        pltpu.make_async_copy(blocks.at[0], b.at[0], sems.at[1]),
        pltpu.make_async_copy(history.at[1], h.at[1], sems.at[2]),
        pltpu.make_async_copy(blocks.at[1], b.at[1], sems.at[3]),
        pltpu.make_async_copy(inverse, own, sems.at[4]),
        pltpu.make_async_copy(excitation, e, sems.at[5]),
    ]
    for load in loads:
        load.start()
    nw, depth, _ = out.shape
    cw = depth - own.shape[0]
    loads[0].wait()
    loads[1].wait()
    stores = []
    for k, piece in enumerate(pieces):
        rows = b.at[0, (k + 1) * cut : (k + 2) * cut]
        stores.append(pltpu.make_async_copy(rows, piece, sems.at[8 + k]))
        stores[-1].start()
    total = mm(b[0], h[0])
    loads[2].wait()
    loads[3].wait()
    total = total + mm(b[1], h[1])
    loads[4].wait()
    loads[5].wait()
    total = less_field(total, e[0])
    for w in range(nw):
        o[w, :cw] = total[w * cw : (w + 1) * cw]
        o[w, cw:] = own[...]
    stores.append(pltpu.make_async_copy(o, out, sems.at[6]))
    stores[-1].start()
    f[...] = less_field(jnp.zeros_like(e[1]), e[1])
    stores.append(pltpu.make_async_copy(f, lead, sems.at[7]))
    stores[-1].start()
    for store in stores:
        store.wait()


def later_sums(blocks, before, history, out):
    out[...] = (mm(blocks[1], history[0]) + mm(blocks[0], before[...])).T


def second_step(got, blocks, *rest):
    sources, (out, piece, sem) = rest[:-3], rest[-3:]
    sources = (blocks.at[0, : piece.shape[0]], *sources)
    for k, source in zip((0,) + ORDER, sources):

        @pl.when(lax.axis_index("x") == k)
        def _():
            pltpu.make_async_copy(source, piece, sem).start()

    ny, depth, span = out.shape
    cw = (depth - piece.shape[0]) // 2
    high, low = parts(sum_first(got, 0, cw))
    for y in range(ny):
        out[y, :cw] = high
        out[y, cw : 2 * cw] = low
    pltpu.make_async_copy(sources[0], piece, sem).wait()
    for y in range(ny):
        out[y, 2 * cw :] = piece[:, y * span : (y + 1) * span]


def third_step(got, later, lead, out):
    nw = out.shape[0]
    cw = later.shape[0] // nw
    total = later[...] + lead[...]
    for w in range(nw):
        high, low = parts(total[w * cw : (w + 1) * cw])
        out[w, :cw] = high
        out[w, cw : 2 * cw] = low
        out[w, 2 * cw :] = got[0, 2 * cw :]


def fourth_step(got1, got2, got3, out, part1, first):
    nz, cw, rows = out.shape
    inverse = got1[:, cw:].reshape(-1, rows)
    term = -mm_t(sum_pairs(got2, 0, cw), inverse, lax.Precision.HIGHEST)
    for z in range(nz):
        out[z] = term
    part1[...] = sum_pairs(got3, 0, cw)
    cut = got3.shape[1] - 2 * cw
    for x in range(first.shape[0] // cut):
        first[x * cut : (x + 1) * cut] = got3[2 * x, 2 * cw :]


def fifth_step(got, part1, first, out, mine):
    value = sum_first(got, 0, got.shape[1])
    total = part1[...] + mm_t(value.astype(BF16), first[...])
    for y in range(out.shape[0]):
        out[y] = total
    cz = mine.shape[0]
    share = value[:cz]
    for z in range(1, value.shape[0] // cz):
        share = jnp.where(lax.axis_index("row") == z, value[z * cz : (z + 1) * cz], share)
    mine[...] = share


def sixth_step(got1, got, mine, out):
    cw = got.shape[1]
    inverse = got1[:, cw:].reshape(-1, got.shape[2])
    out[:cw] = -mm_t(sum_first(got, 0, cw), inverse, lax.Precision.HIGHEST)
    out[cw:] = mine[...]


def shards(blocks, history, excitation, self_inverse):
    ny, nx, nc, nz = (lax.axis_size(a) for a in ("y", "x", "core", "row"))
    nw = nx * nc
    rows, size = blocks.shape[1:]
    columns = history.shape[2]
    cw = columns // nw
    own = self_inverse.shape[0]
    nlag = ny * nw
    cut = rows // nx
    span = nw * own
    work = 2 * rows * size * columns * 2
    small = 2 * cw * rows * span

    before = call(
        last_of,
        (history.shape[1:], BF16),
        0,
        history,
        scratch=[pltpu.SemaphoreType.DMA((4,))],
        held=[pltpu.HBM],
        limit=60,
    )
    before = lax.ppermute(before, LAG, [(i, i + 1) for i in range(nlag - 1)])
    later = call(later_sums, ((columns, rows), F32), work, blocks, before, history)

    outs = [((nw, cw + own, rows), F32), ((columns, rows), F32)] + [((cut, size), BF16)] * (nx - 1)
    scratch = [pltpu.VMEM(blocks.shape, BF16), pltpu.VMEM(history.shape, BF16)]
    scratch += [pltpu.VMEM(excitation.shape, F32), pltpu.VMEM((own, rows), F32)]
    scratch += [pltpu.VMEM(*o) for o in outs[:2]] + [pltpu.SemaphoreType.DMA((8 + nx,))]
    args = blocks, history, excitation, self_inverse
    held, given = [pltpu.HBM] * len(args), [pltpu.HBM] * len(outs)
    send, lead, *pieces = call(
        first_sums, outs, work, *args, scratch=scratch, held=held, given=given, limit=60
    )
    got1 = swap(send, W)
    pieces = [lax.ppermute(pieces[k - 1], LAG, [(0, k * nc), (1, 0)]) for k in ORDER]
    got1, later = lax.optimization_barrier((got1, later))
    send = call(
        second_step,
        ((ny, 2 * cw + cut, span), BF16),
        small,
        got1,
        blocks,
        *pieces,
        scratch=[pltpu.VMEM((cut, size), BF16), pltpu.SemaphoreType.DMA(())],
        held=[pltpu.VMEM] + [pltpu.HBM] * nx,
    )
    got2 = swap(send, "y")
    send = call(third_step, ((nw, 2 * cw + cut, rows), BF16), small, got2, later, lead)
    got3 = swap(send, W)
    outs = [((nz, cw, rows), F32), ((cw, rows), F32), ((rows, span), BF16)]
    send, part1, first = call(fourth_step, outs, small, got1, got2, got3)
    got4 = swap(send, "row")
    cz = cw // nz
    outs = [((ny, cw, rows), F32), ((cz, span), F32)]
    send, mine0 = call(fifth_step, outs, small, got4, part1, first)
    got5 = swap(send, "y")
    both = call(sixth_step, ((cw + cz, span), F32), small, got1, got5, mine0)
    both = both.reshape(cw + cz, nw, own).transpose(1, 0, 2).reshape(nw, 1, (cw + cz) * own)
    both = jnp.broadcast_to(both, (nw, nz, (cw + cz) * own)).reshape(nw * nz, (cw + cz) * own)
    got = swap(both, W + ("row",)).reshape(nw, nz, cw + cz, own)
    out1 = jnp.sum(got[:, :, :cw], axis=1).reshape(columns, own)
    out0 = got[:, :, cw:].reshape(columns, own)
    return jnp.stack([out0.T, out1.T])


def solution(mesh):
    n_row = mesh.shape["row"]
    fine = Mesh(np.asarray(mesh.devices).reshape(-1, 4, 2, n_row), ("y", "x", "core", "row"))
    return jax.shard_map(
        shards,
        mesh=fine,
        in_specs=(
            P(LAG, "row", None),
            P(LAG, None, None),
            P(None, "row", None),
            P(LAG, "row"),
        ),
        out_specs=P(None, LAG, None),
        check_vma=False,
    )
```

```python
import numpy as np
import jax
import jax.numpy as jnp
from jax import lax
from jax.experimental import pallas as pl
from jax.experimental.pallas import tpu as pltpu
from jax.sharding import Mesh, PartitionSpec as P

LAG = ("y", "x", "core")
W = ("x", "core")
ORDER = (2, 3, 1)
F32 = jnp.float32
BF16 = jnp.bfloat16


def swap(pieces, axes):
    return lax.all_to_all(pieces, axes, 0, 0, tiled=True)


def call(body, outs, flops, *args, scratch=(), held=None, given=None, limit=24):
    single = not isinstance(outs, list)
    outs = [outs] if single else outs
    shapes = [jax.ShapeDtypeStruct(s, d) for s, d in outs]
    size = sum(a.size * a.dtype.itemsize for a in args)
    size += sum(s.size * s.dtype.itemsize for s in shapes)
    held = held or [pltpu.VMEM] * len(args)
    given = given or [pltpu.VMEM] * len(outs)
    specs = [pl.BlockSpec(memory_space=m) for m in given]
    return pl.pallas_call(
        body,
        out_shape=shapes[0] if single else shapes,
        in_specs=[pl.BlockSpec(memory_space=m) for m in held],
        out_specs=specs[0] if single else specs,
        scratch_shapes=scratch,
        cost_estimate=pl.CostEstimate(flops=flops, bytes_accessed=size, transcendentals=0),
        compiler_params=pltpu.CompilerParams(vmem_limit_bytes=limit * 1024 * 1024),
    )(*args)


def mm(left, right, precision=None):
    return jnp.dot(left, right, precision=precision, preferred_element_type=F32)


def mm_t(left, right, precision=None):
    return lax.dot_general(
        left, right, (((1,), (1,)), ((), ())), precision=precision, preferred_element_type=F32
    )


def parts(array):
    high = array.astype(BF16)
    return high, (array - high.astype(F32)).astype(BF16)


def sum_first(ref, start, stop):
    total = ref[0, start:stop].astype(F32)
    for i in range(1, ref.shape[0]):
        total = total + ref[i, start:stop].astype(F32)
    return total


def sum_pairs(ref, start, count):
    return sum_first(ref, start, start + count) + sum_first(ref, start + count, start + 2 * count)


def less_field(total, field):
    return jnp.where(lax.axis_index(LAG) == 0, total - field, total).T


def own_copies(history, blocks, out_h, out_b, held_h, held_b, sems):
    moves = []
    for j, (source, held, out) in enumerate(
        ((blocks.at[0, out_b.shape[0] :], held_b, out_b), (history.at[1], held_h, out_h))
    ):
        count = sems.shape[2]
        step = out.shape[0] // count
        for i in range(count):
            rows = pl.ds(i * step, step)
            load = pltpu.make_async_copy(source.at[rows], held.at[rows], sems.at[0, j, i])
            store = pltpu.make_async_copy(held.at[rows], out.at[rows], sems.at[1, j, i])
            moves.append((load, store))
            load.start()
    for load, store in moves:
        load.wait()
        store.start()
    for _, store in moves:
        store.wait()


def first_sums(blocks, history, excitation, inverse, half, out, lead, *rest):
    pieces, (b, h, e, own, o, f, g, sems) = rest[:-8], rest[-8:]
    cut = pieces[0].shape[0]
    loads = [
        pltpu.make_async_copy(history.at[0], h.at[0], sems.at[0]),
        pltpu.make_async_copy(blocks.at[0], b.at[0], sems.at[1]),
        pltpu.make_async_copy(history.at[1], h.at[1], sems.at[2]),
        pltpu.make_async_copy(blocks.at[1], b.at[1], sems.at[3]),
        pltpu.make_async_copy(inverse, own, sems.at[4]),
        pltpu.make_async_copy(excitation, e, sems.at[5]),
        pltpu.make_async_copy(half, g, sems.at[6]),
    ]
    for load in loads:
        load.start()
    nw, depth, _ = out.shape
    cw = depth - own.shape[0]
    loads[0].wait()
    loads[1].wait()
    total = mm(b[0], h[0])
    loads[6].wait()
    for core, source in enumerate((b.at[0, : g.shape[0]], g)):

        @pl.when(lax.axis_index("core") == core)
        def _():
            for k, piece in enumerate(pieces):
                rows = source.at[k * cut : (k + 1) * cut]
                pltpu.make_async_copy(rows, piece, sems.at[9 + k]).start()

    loads[2].wait()
    loads[3].wait()
    total = total + mm(b[1], h[1])
    loads[4].wait()
    loads[5].wait()
    total = less_field(total, e[0])
    for w in range(nw):
        o[w, :cw] = total[w * cw : (w + 1) * cw]
        o[w, cw:] = own[...]
    stores = [pltpu.make_async_copy(o, out, sems.at[7])]
    stores[-1].start()
    f[...] = less_field(jnp.zeros_like(e[1]), e[1])
    stores.append(pltpu.make_async_copy(f, lead, sems.at[8]))
    stores[-1].start()
    for k, piece in enumerate(pieces):
        rows = g.at[k * cut : (k + 1) * cut]
        stores.append(pltpu.make_async_copy(rows, piece, sems.at[9 + k]))
    for store in stores:
        store.wait()


def later_sums(blocks, before, history, lead, out):
    out[...] = (mm(blocks[1], history[0]) + mm(blocks[0], before[...])).T + lead[...]


def second_step(got, *rest):
    sources, (out, piece, sem) = rest[:-3], rest[-3:]
    for k, source in zip((0,) + ORDER, sources):

        @pl.when(lax.axis_index("x") == k)
        def _():
            pltpu.make_async_copy(source, piece, sem).start()

    ny, depth, span = out.shape
    cw = (depth - piece.shape[0]) // 2
    high, low = parts(sum_first(got, 0, cw))
    for y in range(ny):
        out[y, :cw] = high
        out[y, cw : 2 * cw] = low
    pltpu.make_async_copy(sources[0], piece, sem).wait()
    for y in range(ny):
        out[y, 2 * cw :] = piece[:, y * span : (y + 1) * span]


def third_step(got, later, out):
    nw = out.shape[0]
    cw = later.shape[0] // nw
    for w in range(nw):
        high, low = parts(later[w * cw : (w + 1) * cw])
        out[w, :cw] = high
        out[w, cw : 2 * cw] = low
        out[w, 2 * cw :] = got[0, 2 * cw :]


def fourth_step(got1, got2, got3, out, part1, first):
    nz, cw, rows = out.shape
    inverse = got1[:, cw:].reshape(-1, rows)
    term = -mm_t(sum_pairs(got2, 0, cw), inverse, lax.Precision.HIGHEST)
    for z in range(nz):
        out[z] = term
    part1[...] = sum_pairs(got3, 0, cw)
    nw, depth, _ = got3.shape
    cut = depth - 2 * cw
    for x in range(nw // 2):
        for core in range(2):
            start = (core * nw // 2 + x) * cut
            first[start : start + cut] = got3[2 * x + core, 2 * cw :]


def fifth_step(got, part1, first, out, mine):
    value = sum_first(got, 0, got.shape[1])
    total = part1[...] + mm_t(value.astype(BF16), first[...])
    for y in range(out.shape[0]):
        out[y] = total
    cz = mine.shape[0]
    share = value[:cz]
    for z in range(1, value.shape[0] // cz):
        share = jnp.where(lax.axis_index("row") == z, value[z * cz : (z + 1) * cz], share)
    mine[...] = share


def sixth_step(got1, got, mine, out):
    cw = got.shape[1]
    inverse = got1[:, cw:].reshape(-1, got.shape[2])
    out[:cw] = -mm_t(sum_first(got, 0, cw), inverse, lax.Precision.HIGHEST)
    out[cw:] = mine[...]


def shards(blocks, history, excitation, self_inverse):
    ny, nx, nc, nz = (lax.axis_size(a) for a in ("y", "x", "core", "row"))
    nw = nx * nc
    rows, size = blocks.shape[1:]
    columns = history.shape[2]
    cw = columns // nw
    own = self_inverse.shape[0]
    nlag = ny * nw
    cut = rows // nw
    span = nw * own
    work = 2 * rows * size * columns * 2
    small = 2 * cw * rows * span

    part = (rows // nc, size)
    before, half = call(
        own_copies,
        [(history.shape[1:], BF16), (part, BF16)],
        0,
        history,
        blocks,
        scratch=[
            pltpu.VMEM(history.shape[1:], BF16),
            pltpu.VMEM(part, BF16),
            pltpu.SemaphoreType.DMA((2, 2, 4)),
        ],
        held=[pltpu.HBM] * 2,
        given=[pltpu.HBM] * 2,
        limit=60,
    )
    half = lax.ppermute(half, LAG, [(i, i ^ 1) for i in range(nlag)])
    before = lax.ppermute(before, LAG, [(i, i + 1) for i in range(nlag - 1)])

    outs = [((nw, cw + own, rows), F32), ((columns, rows), F32)] + [((cut, size), BF16)] * nx
    scratch = [pltpu.VMEM(blocks.shape, BF16), pltpu.VMEM(history.shape, BF16)]
    scratch += [pltpu.VMEM(excitation.shape, F32), pltpu.VMEM((own, rows), F32)]
    scratch += [pltpu.VMEM(*o) for o in outs[:2]] + [pltpu.VMEM(part, BF16)]
    scratch += [pltpu.SemaphoreType.DMA((9 + nx,))]
    args = blocks, history, excitation, self_inverse, half
    held, given = [pltpu.HBM] * len(args), [pltpu.HBM] * len(outs)
    send, lead, *pieces = call(
        first_sums, outs, work, *args, scratch=scratch, held=held, given=given, limit=60
    )
    got1 = swap(send, W)
    routes = {k: [(c, k * nc + c) for c in range(nc)] for k in ORDER}
    sent = [lax.ppermute(pieces[k], LAG, routes[k]) for k in ORDER]
    later = call(later_sums, ((columns, rows), F32), work, blocks, before, history, lead)
    got1, later = lax.optimization_barrier((got1, later))
    send = call(
        second_step,
        ((ny, 2 * cw + cut, span), BF16),
        small,
        got1,
        pieces[0],
        *sent,
        scratch=[pltpu.VMEM((cut, size), BF16), pltpu.SemaphoreType.DMA(())],
        held=[pltpu.VMEM] + [pltpu.HBM] * nx,
    )
    got2 = swap(send, "y")
    send = call(third_step, ((nw, 2 * cw + cut, rows), BF16), small, got2, later)
    got3 = swap(send, W)
    outs = [((nz, cw, rows), F32), ((cw, rows), F32), ((rows, span), BF16)]
    send, part1, first = call(fourth_step, outs, small, got1, got2, got3)
    got4 = swap(send, "row")
    cz = cw // nz
    outs = [((ny, cw, rows), F32), ((cz, span), F32)]
    send, mine0 = call(fifth_step, outs, small, got4, part1, first)
    got5 = swap(send, "y")
    both = call(sixth_step, ((cw + cz, span), F32), small, got1, got5, mine0)
    both = both.reshape(cw + cz, nw, own).transpose(1, 0, 2).reshape(nw, 1, (cw + cz) * own)
    both = jnp.broadcast_to(both, (nw, nz, (cw + cz) * own)).reshape(nw * nz, (cw + cz) * own)
    got = swap(both, W + ("row",)).reshape(nw, nz, cw + cz, own)
    out1 = jnp.sum(got[:, :, :cw], axis=1).reshape(columns, own)
    out0 = got[:, :, cw:].reshape(columns, own)
    return jnp.stack([out0.T, out1.T])


def solution(mesh):
    n_row = mesh.shape["row"]
    fine = Mesh(np.asarray(mesh.devices).reshape(-1, 4, 2, n_row), ("y", "x", "core", "row"))
    return jax.shard_map(
        shards,
        mesh=fine,
        in_specs=(
            P(LAG, "row", None),
            P(LAG, None, None),
            P(None, "row", None),
            P(LAG, "row"),
        ),
        out_specs=P(None, LAG, None),
        check_vma=False,
    )
```

```python
import functools

import numpy as np
import jax
import jax.numpy as jnp
from jax import lax
from jax.experimental import pallas as pl
from jax.experimental.pallas import tpu as pltpu
from jax.sharding import Mesh, PartitionSpec as P

LAG = ("y", "x", "core")
W = ("x", "core")
HOLDERS = (0, 6, 2, 1)
F32 = jnp.float32
BF16 = jnp.bfloat16


def swap(pieces, axes):
    return lax.all_to_all(pieces, axes, 0, 0, tiled=True)


def call(body, outs, flops, *args, scratch=(), held=None, given=None, limit=24):
    single = not isinstance(outs, list)
    outs = [outs] if single else outs
    shapes = [jax.ShapeDtypeStruct(s, d) for s, d in outs]
    size = sum(a.size * a.dtype.itemsize for a in args)
    size += sum(s.size * s.dtype.itemsize for s in shapes)
    held = held or [pltpu.VMEM] * len(args)
    given = given or [pltpu.VMEM] * len(outs)
    specs = [pl.BlockSpec(memory_space=m) for m in given]
    return pl.pallas_call(
        body,
        out_shape=shapes[0] if single else shapes,
        in_specs=[pl.BlockSpec(memory_space=m) for m in held],
        out_specs=specs[0] if single else specs,
        scratch_shapes=scratch,
        cost_estimate=pl.CostEstimate(flops=flops, bytes_accessed=size, transcendentals=0),
        compiler_params=pltpu.CompilerParams(vmem_limit_bytes=limit * 1024 * 1024),
    )(*args)


def mm(left, right, precision=None):
    return jnp.dot(left, right, precision=precision, preferred_element_type=F32)


def mm_t(left, right, precision=None):
    return lax.dot_general(
        left, right, (((1,), (1,)), ((), ())), precision=precision, preferred_element_type=F32
    )


def parts(array):
    high = array.astype(BF16)
    return high, (array - high.astype(F32)).astype(BF16)


def sum_first(ref, start, stop):
    total = ref[0, start:stop].astype(F32)
    for i in range(1, ref.shape[0]):
        total = total + ref[i, start:stop].astype(F32)
    return total


def sum_pairs(ref, start, count):
    return sum_first(ref, start, start + count) + sum_first(ref, start + count, start + 2 * count)


def less_field(total, field):
    return jnp.where(lax.axis_index(LAG) == 0, total - field, total).T


def last_of(history, out, held, sems):
    count = sems.shape[1]
    step = out.shape[0] // count
    moves = []
    for i in range(count):
        rows = pl.ds(i * step, step)
        load = pltpu.make_async_copy(history.at[1, rows], held.at[rows], sems.at[0, i])
        moves.append((load, pltpu.make_async_copy(held.at[rows], out.at[rows], sems.at[1, i])))
        load.start()
    for load, store in moves:
        load.wait()
        store.start()
    for _, store in moves:
        store.wait()


def first_sums(blocks, history, excitation, inverse, out, lead, *rest):
    pieces, (b, h, e, own, o, f, sems) = rest[:-7], rest[-7:]
    cut = pieces[0].shape[0]
    loads = [
        pltpu.make_async_copy(history.at[0], h.at[0], sems.at[0]),
        pltpu.make_async_copy(blocks.at[0], b.at[0], sems.at[1]),
        pltpu.make_async_copy(history.at[1], h.at[1], sems.at[2]),
        pltpu.make_async_copy(blocks.at[1], b.at[1], sems.at[3]),
        pltpu.make_async_copy(inverse, own, sems.at[4]),
        pltpu.make_async_copy(excitation, e, sems.at[5]),
    ]
    for load in loads:
        load.start()
    nw, depth, _ = out.shape
    cw = depth - own.shape[0]
    loads[0].wait()
    loads[1].wait()
    stores = []
    for k, piece in enumerate(pieces):
        rows = b.at[0, (k + 1) * cut : (k + 2) * cut]
        stores.append(pltpu.make_async_copy(rows, piece, sems.at[8 + k]))
        stores[-1].start()
    total = mm(b[0], h[0])
    loads[2].wait()
    loads[3].wait()
    total = total + mm(b[1], h[1])
    loads[4].wait()
    loads[5].wait()
    total = less_field(total, e[0])
    for w in range(nw):
        o[w, :cw] = total[w * cw : (w + 1) * cw]
        o[w, cw:] = own[...]
    stores.append(pltpu.make_async_copy(o, out, sems.at[6]))
    stores[-1].start()
    f[...] = less_field(jnp.zeros_like(e[1]), e[1])
    stores.append(pltpu.make_async_copy(f, lead, sems.at[7]))
    stores[-1].start()
    for store in stores:
        store.wait()


def later_sums(blocks, before, history, out):
    out[...] = (mm(blocks[1], history[0]) + mm(blocks[0], before[...])).T


def second_step(got, blocks, *rest):
    sources, (out, piece, sem) = rest[:-3], rest[-3:]
    sources = (blocks.at[0, : piece.shape[0]], *sources)
    w = lax.axis_index(W)
    for k, source in zip(HOLDERS[:-1], sources):

        @pl.when(w == k)
        def _():
            pltpu.make_async_copy(source, piece, sem).start()

    @pl.when(functools.reduce(jnp.logical_and, [w != k for k in HOLDERS[:-1]]))
    def _():
        pltpu.make_async_copy(sources[-1], piece, sem).start()

    ny, depth, span = out.shape
    cw = (depth - piece.shape[0]) // 2
    high, low = parts(sum_first(got, 0, cw))
    for y in range(ny):
        out[y, :cw] = high
        out[y, cw : 2 * cw] = low
    pltpu.make_async_copy(sources[0], piece, sem).wait()
    for y in range(ny):
        out[y, 2 * cw :] = piece[:, y * span : (y + 1) * span]


def third_step(got, later, lead, out):
    nw = out.shape[0]
    cw = later.shape[0] // nw
    total = later[...] + lead[...]
    for w in range(nw):
        high, low = parts(total[w * cw : (w + 1) * cw])
        out[w, :cw] = high
        out[w, cw : 2 * cw] = low
        out[w, 2 * cw :] = got[0, 2 * cw :]


def fourth_step(got1, got2, got3, out, part1, first):
    nz, cw, rows = out.shape
    inverse = got1[:, cw:].reshape(-1, rows)
    term = -mm_t(sum_pairs(got2, 0, cw), inverse, lax.Precision.HIGHEST)
    for z in range(nz):
        out[z] = term
    part1[...] = sum_pairs(got3, 0, cw)
    cut = got3.shape[1] - 2 * cw
    for i, w in enumerate(HOLDERS):
        first[i * cut : (i + 1) * cut] = got3[w, 2 * cw :]


def fifth_step(got, part1, first, out, mine):
    value = sum_first(got, 0, got.shape[1])
    total = part1[...] + mm_t(value.astype(BF16), first[...])
    for y in range(out.shape[0]):
        out[y] = total
    cz = mine.shape[0]
    share = value[:cz]
    for z in range(1, value.shape[0] // cz):
        share = jnp.where(lax.axis_index("row") == z, value[z * cz : (z + 1) * cz], share)
    mine[...] = share


def sixth_step(got1, got, mine, out):
    cw = got.shape[1]
    inverse = got1[:, cw:].reshape(-1, got.shape[2])
    out[:cw] = -mm_t(sum_first(got, 0, cw), inverse, lax.Precision.HIGHEST)
    out[cw:] = mine[...]


def shards(blocks, history, excitation, self_inverse):
    ny, nx, nc, nz = (lax.axis_size(a) for a in ("y", "x", "core", "row"))
    nw = nx * nc
    rows, size = blocks.shape[1:]
    columns = history.shape[2]
    cw = columns // nw
    own = self_inverse.shape[0]
    nlag = ny * nw
    cut = rows // len(HOLDERS)
    span = nw * own
    work = 2 * rows * size * columns * 2
    small = 2 * cw * rows * span

    before = call(
        last_of,
        (history.shape[1:], BF16),
        0,
        history,
        scratch=[pltpu.VMEM(history.shape[1:], BF16), pltpu.SemaphoreType.DMA((2, 4))],
        held=[pltpu.HBM],
        given=[pltpu.HBM],
        limit=60,
    )
    before = lax.ppermute(before, LAG, [(i, i + 1) for i in range(nlag - 1)])
    later = call(later_sums, ((columns, rows), F32), work, blocks, before, history)

    outs = [((nw, cw + own, rows), F32), ((columns, rows), F32)] + [((cut, size), BF16)] * (len(HOLDERS) - 1)
    scratch = [pltpu.VMEM(blocks.shape, BF16), pltpu.VMEM(history.shape, BF16)]
    scratch += [pltpu.VMEM(excitation.shape, F32), pltpu.VMEM((own, rows), F32)]
    scratch += [pltpu.VMEM(*o) for o in outs[:2]] + [pltpu.SemaphoreType.DMA((7 + len(HOLDERS),))]
    args = blocks, history, excitation, self_inverse
    held, given = [pltpu.HBM] * len(args), [pltpu.HBM] * len(outs)
    send, lead, *pieces = call(
        first_sums, outs, work, *args, scratch=scratch, held=held, given=given, limit=60
    )
    got1 = swap(send, W)
    pieces = [lax.ppermute(p, LAG, [(0, w)]) for p, w in zip(pieces, HOLDERS[1:])]
    got1, later = lax.optimization_barrier((got1, later))
    send = call(
        second_step,
        ((ny, 2 * cw + cut, span), BF16),
        small,
        got1,
        blocks,
        *pieces,
        scratch=[pltpu.VMEM((cut, size), BF16), pltpu.SemaphoreType.DMA(())],
        held=[pltpu.VMEM] + [pltpu.HBM] * len(HOLDERS),
    )
    got2 = swap(send, "y")
    send = call(third_step, ((nw, 2 * cw + cut, rows), BF16), small, got2, later, lead)
    got3 = swap(send, W)
    outs = [((nz, cw, rows), F32), ((cw, rows), F32), ((rows, span), BF16)]
    send, part1, first = call(fourth_step, outs, small, got1, got2, got3)
    got4 = swap(send, "row")
    cz = cw // nz
    outs = [((ny, cw, rows), F32), ((cz, span), F32)]
    send, mine0 = call(fifth_step, outs, small, got4, part1, first)
    got5 = swap(send, "y")
    both = call(sixth_step, ((cw + cz, span), F32), small, got1, got5, mine0)
    both = both.reshape(cw + cz, nw, own).transpose(1, 0, 2).reshape(nw, 1, (cw + cz) * own)
    both = jnp.broadcast_to(both, (nw, nz, (cw + cz) * own)).reshape(nw * nz, (cw + cz) * own)
    got = swap(both, W + ("row",)).reshape(nw, nz, cw + cz, own)
    out1 = jnp.sum(got[:, :, :cw], axis=1).reshape(columns, own)
    out0 = got[:, :, cw:].reshape(columns, own)
    return jnp.stack([out0.T, out1.T])


def solution(mesh):
    n_row = mesh.shape["row"]
    fine = Mesh(np.asarray(mesh.devices).reshape(-1, 4, 2, n_row), ("y", "x", "core", "row"))
    return jax.shard_map(
        shards,
        mesh=fine,
        in_specs=(
            P(LAG, "row", None),
            P(LAG, None, None),
            P(None, "row", None),
            P(LAG, "row"),
        ),
        out_specs=P(None, LAG, None),
        check_vma=False,
    )
```

```python
import numpy as np
import jax
import jax.numpy as jnp
from jax import lax
from jax.experimental import pallas as pl
from jax.experimental.pallas import tpu as pltpu
from jax.sharding import Mesh, PartitionSpec as P

LAG = ("y", "x", "core")
W = ("x", "core")
ORDER = (2, 3, 1)
F32 = jnp.float32
BF16 = jnp.bfloat16


def swap(pieces, axes):
    return lax.all_to_all(pieces, axes, 0, 0, tiled=True)


def call(body, outs, flops, *args, scratch=(), held=None, given=None, limit=24):
    single = not isinstance(outs, list)
    outs = [outs] if single else outs
    shapes = [jax.ShapeDtypeStruct(s, d) for s, d in outs]
    size = sum(a.size * a.dtype.itemsize for a in args)
    size += sum(s.size * s.dtype.itemsize for s in shapes)
    held = held or [pltpu.VMEM] * len(args)
    given = given or [pltpu.VMEM] * len(outs)
    specs = [pl.BlockSpec(memory_space=m) for m in given]
    return pl.pallas_call(
        body,
        out_shape=shapes[0] if single else shapes,
        in_specs=[pl.BlockSpec(memory_space=m) for m in held],
        out_specs=specs[0] if single else specs,
        scratch_shapes=scratch,
        cost_estimate=pl.CostEstimate(flops=flops, bytes_accessed=size, transcendentals=0),
        compiler_params=pltpu.CompilerParams(vmem_limit_bytes=limit * 1024 * 1024),
    )(*args)


def mm(left, right, precision=None):
    return jnp.dot(left, right, precision=precision, preferred_element_type=F32)


def mm_t(left, right, precision=None):
    return lax.dot_general(
        left, right, (((1,), (1,)), ((), ())), precision=precision, preferred_element_type=F32
    )


def parts(array):
    high = array.astype(BF16)
    return high, (array - high.astype(F32)).astype(BF16)


def sum_first(ref, start, stop):
    total = ref[0, start:stop].astype(F32)
    for i in range(1, ref.shape[0]):
        total = total + ref[i, start:stop].astype(F32)
    return total


def sum_pairs(ref, start, count):
    return sum_first(ref, start, start + count) + sum_first(ref, start + count, start + 2 * count)


def less_field(total, field):
    return jnp.where(lax.axis_index(LAG) == 0, total - field, total).T


def own_copies(history, blocks, out_h, out_b, held_h, held_b, sems):
    moves = []
    for j, (source, held, out) in enumerate(
        ((blocks.at[0, out_b.shape[0] :], held_b, out_b), (history.at[1], held_h, out_h))
    ):
        count = sems.shape[2]
        step = out.shape[0] // count
        for i in range(count):
            rows = pl.ds(i * step, step)
            load = pltpu.make_async_copy(source.at[rows], held.at[rows], sems.at[0, j, i])
            store = pltpu.make_async_copy(held.at[rows], out.at[rows], sems.at[1, j, i])
            moves.append((load, store))
            load.start()
    for load, store in moves:
        load.wait()
        store.start()
    for _, store in moves:
        store.wait()


def first_sums(blocks, history, excitation, inverse, half, out, field, *rest):
    pieces, (b, h, e, own, turned, o, f, g, sems) = rest[:-9], rest[-9:]
    cut = pieces[0].shape[0]
    loads = [
        pltpu.make_async_copy(history.at[0], h.at[0], sems.at[0]),
        pltpu.make_async_copy(blocks.at[0], b.at[0], sems.at[1]),
        pltpu.make_async_copy(history.at[1], h.at[1], sems.at[2]),
        pltpu.make_async_copy(blocks.at[1], b.at[1], sems.at[3]),
        pltpu.make_async_copy(inverse, own, sems.at[4]),
        pltpu.make_async_copy(excitation, e, sems.at[5]),
        pltpu.make_async_copy(half, g, sems.at[6]),
    ]
    for load in loads:
        load.start()
    nw, depth, _ = out.shape
    cw = depth - own.shape[0]
    loads[0].wait()
    loads[1].wait()
    total = mm(b[0], h[0])
    loads[6].wait()
    for core, source in enumerate((b.at[0, : g.shape[0]], g)):

        @pl.when(lax.axis_index("core") == core)
        def _():
            for k, piece in enumerate(pieces):
                rows = source.at[k * cut : (k + 1) * cut]
                pltpu.make_async_copy(rows, piece, sems.at[9 + k]).start()

    loads[2].wait()
    loads[3].wait()
    total = total + mm(b[1], h[1])
    loads[4].wait()
    loads[5].wait()
    total = less_field(total, e[0])
    for w in range(nw):
        o[w, :cw] = total[w * cw : (w + 1) * cw]
        o[w, cw:] = own[...]
    stores = [pltpu.make_async_copy(o, out, sems.at[7])]
    stores[-1].start()
    turned[...] = e[1].T
    f[...] = turned[pl.ds(pl.multiple_of(lax.axis_index(W) * cw, cw), cw)]
    stores.append(pltpu.make_async_copy(f, field, sems.at[8]))
    stores[-1].start()
    for k, piece in enumerate(pieces):
        rows = g.at[k * cut : (k + 1) * cut]
        stores.append(pltpu.make_async_copy(rows, piece, sems.at[9 + k]))
    for store in stores:
        store.wait()


def later_sums(blocks, before, history, out):
    out[...] = (mm(blocks[1], history[0]) + mm(blocks[0], before[...])).T


def second_step(got, *rest):
    sources, (out, piece, sem) = rest[:-3], rest[-3:]
    for k, source in zip((0,) + ORDER, sources):

        @pl.when(lax.axis_index("x") == k)
        def _():
            pltpu.make_async_copy(source, piece, sem).start()

    ny, depth, span = out.shape
    cw = (depth - piece.shape[0]) // 2
    high, low = parts(sum_first(got, 0, cw))
    for y in range(ny):
        out[y, :cw] = high
        out[y, cw : 2 * cw] = low
    pltpu.make_async_copy(sources[0], piece, sem).wait()
    for y in range(ny):
        out[y, 2 * cw :] = piece[:, y * span : (y + 1) * span]


def third_step(got, later, out):
    nw = out.shape[0]
    cw = later.shape[0] // nw
    for w in range(nw):
        high, low = parts(later[w * cw : (w + 1) * cw])
        out[w, :cw] = high
        out[w, cw : 2 * cw] = low
        out[w, 2 * cw :] = got[0, 2 * cw :]


def fourth_step(got1, got2, got3, out, part1, first):
    nz, cw, rows = out.shape
    inverse = got1[:, cw:].reshape(-1, rows)
    term = -mm_t(sum_pairs(got2, 0, cw), inverse, lax.Precision.HIGHEST)
    for z in range(nz):
        out[z] = term
    part1[...] = sum_pairs(got3, 0, cw)
    nw, depth, _ = got3.shape
    cut = depth - 2 * cw
    for x in range(nw // 2):
        for core in range(2):
            start = (core * nw // 2 + x) * cut
            first[start : start + cut] = got3[2 * x + core, 2 * cw :]


def fifth_step(got, part1, first, out, mine):
    value = sum_first(got, 0, got.shape[1])
    total = part1[...] + mm_t(value.astype(BF16), first[...])
    for y in range(out.shape[0]):
        out[y] = total
    cz = mine.shape[0]
    share = value[:cz]
    for z in range(1, value.shape[0] // cz):
        share = jnp.where(lax.axis_index("row") == z, value[z * cz : (z + 1) * cz], share)
    mine[...] = share


def sixth_step(got1, got, field, mine, out):
    cw = got.shape[1]
    inverse = got1[:, cw:].reshape(-1, got.shape[2])
    resid = field[...] - sum_first(got, 0, cw)
    out[:cw] = mm_t(resid, inverse, lax.Precision.HIGHEST)
    out[cw:] = mine[...]


def shards(blocks, history, excitation, self_inverse):
    ny, nx, nc, nz = (lax.axis_size(a) for a in ("y", "x", "core", "row"))
    nw = nx * nc
    rows, size = blocks.shape[1:]
    columns = history.shape[2]
    cw = columns // nw
    own = self_inverse.shape[0]
    nlag = ny * nw
    cut = rows // nw
    span = nw * own
    work = 2 * rows * size * columns * 2
    small = 2 * cw * rows * span

    part = (rows // nc, size)
    before, half = call(
        own_copies,
        [(history.shape[1:], BF16), (part, BF16)],
        0,
        history,
        blocks,
        scratch=[
            pltpu.VMEM(history.shape[1:], BF16),
            pltpu.VMEM(part, BF16),
            pltpu.SemaphoreType.DMA((2, 2, 4)),
        ],
        held=[pltpu.HBM] * 2,
        given=[pltpu.HBM] * 2,
        limit=60,
    )
    half = lax.ppermute(half, LAG, [(i, i ^ 1) for i in range(nlag)])
    before = lax.ppermute(before, LAG, [(i, i + 1) for i in range(nlag - 1)])

    outs = [((nw, cw + own, rows), F32), ((cw, rows), F32)] + [((cut, size), BF16)] * nx
    scratch = [pltpu.VMEM(blocks.shape, BF16), pltpu.VMEM(history.shape, BF16)]
    scratch += [pltpu.VMEM(excitation.shape, F32), pltpu.VMEM((own, rows), F32)]
    scratch += [pltpu.VMEM((columns, rows), F32)]
    scratch += [pltpu.VMEM(*o) for o in outs[:2]] + [pltpu.VMEM(part, BF16)]
    scratch += [pltpu.SemaphoreType.DMA((9 + nx,))]
    args = blocks, history, excitation, self_inverse, half
    held, given = [pltpu.HBM] * len(args), [pltpu.HBM] * len(outs)
    send, field, *pieces = call(
        first_sums, outs, work, *args, scratch=scratch, held=held, given=given, limit=60
    )
    got1 = swap(send, W)
    routes = {k: [(c, k * nc + c) for c in range(nc)] for k in ORDER}
    sent = [lax.ppermute(pieces[k], LAG, routes[k]) for k in ORDER]
    got1, before = lax.optimization_barrier((got1, before))
    later = call(later_sums, ((columns, rows), F32), work, blocks, before, history)
    got1, later = lax.optimization_barrier((got1, later))
    send = call(
        second_step,
        ((ny, 2 * cw + cut, span), BF16),
        small,
        got1,
        pieces[0],
        *sent,
        scratch=[pltpu.VMEM((cut, size), BF16), pltpu.SemaphoreType.DMA(())],
        held=[pltpu.VMEM] + [pltpu.HBM] * nx,
        limit=24,
    )
    got2 = swap(send, "y")
    send = call(third_step, ((nw, 2 * cw + cut, rows), BF16), small, got2, later)
    got3 = swap(send, W)
    outs = [((nz, cw, rows), F32), ((cw, rows), F32), ((rows, span), BF16)]
    send, part1, first = call(fourth_step, outs, small, got1, got2, got3)
    got4 = swap(send, "row")
    cz = cw // nz
    outs = [((ny, cw, rows), F32), ((cz, span), F32)]
    send, mine0 = call(fifth_step, outs, small, got4, part1, first)
    got5 = swap(send, "y")
    both = call(sixth_step, ((cw + cz, span), F32), small, got1, got5, field, mine0)
    both = both.reshape(cw + cz, nw, own).transpose(1, 0, 2).reshape(nw, 1, (cw + cz) * own)
    both = jnp.broadcast_to(both, (nw, nz, (cw + cz) * own)).reshape(nw * nz, (cw + cz) * own)
    got = swap(both, W + ("row",)).reshape(nw, nz, cw + cz, own)
    out1 = jnp.sum(got[:, :, :cw], axis=1).reshape(columns, own)
    out0 = got[:, :, cw:].reshape(columns, own)
    return jnp.stack([out0.T, out1.T])


def solution(mesh):
    n_row = mesh.shape["row"]
    fine = Mesh(np.asarray(mesh.devices).reshape(-1, 4, 2, n_row), ("y", "x", "core", "row"))
    return jax.shard_map(
        shards,
        mesh=fine,
        in_specs=(
            P(LAG, "row", None),
            P(LAG, None, None),
            P(None, "row", None),
            P(LAG, "row"),
        ),
        out_specs=P(None, LAG, None),
        check_vma=False,
    )
```

```python
import functools

import numpy as np
import jax
import jax.numpy as jnp
from jax import lax
from jax.experimental import pallas as pl
from jax.experimental.pallas import tpu as pltpu
from jax.sharding import Mesh, PartitionSpec as P

LAG = ("y", "x", "core")
W = ("x", "core")
HOLDERS = (0, 6, 2, 1)
F32 = jnp.float32
BF16 = jnp.bfloat16


def swap(pieces, axes):
    return lax.all_to_all(pieces, axes, 0, 0, tiled=True)


def call(body, outs, flops, *args, scratch=(), held=None, given=None, limit=24):
    single = not isinstance(outs, list)
    outs = [outs] if single else outs
    shapes = [jax.ShapeDtypeStruct(s, d) for s, d in outs]
    size = sum(a.size * a.dtype.itemsize for a in args)
    size += sum(s.size * s.dtype.itemsize for s in shapes)
    held = held or [pltpu.VMEM] * len(args)
    given = given or [pltpu.VMEM] * len(outs)
    specs = [pl.BlockSpec(memory_space=m) for m in given]
    return pl.pallas_call(
        body,
        out_shape=shapes[0] if single else shapes,
        in_specs=[pl.BlockSpec(memory_space=m) for m in held],
        out_specs=specs[0] if single else specs,
        scratch_shapes=scratch,
        cost_estimate=pl.CostEstimate(flops=flops, bytes_accessed=size, transcendentals=0),
        compiler_params=pltpu.CompilerParams(vmem_limit_bytes=limit * 1024 * 1024),
    )(*args)


def mm(left, right, precision=None):
    return jnp.dot(left, right, precision=precision, preferred_element_type=F32)


def mm_t(left, right, precision=None):
    return lax.dot_general(
        left, right, (((1,), (1,)), ((), ())), precision=precision, preferred_element_type=F32
    )


def parts(array):
    high = array.astype(BF16)
    return high, (array - high.astype(F32)).astype(BF16)


def sum_first(ref, start, stop):
    total = ref[0, start:stop].astype(F32)
    for i in range(1, ref.shape[0]):
        total = total + ref[i, start:stop].astype(F32)
    return total


def sum_pairs(ref, start, count):
    return sum_first(ref, start, start + count) + sum_first(ref, start + count, start + 2 * count)


def less_field(total, field):
    return jnp.where(lax.axis_index(LAG) == 0, total - field, total).T


def first_sums(blocks, history, excitation, inverse, out, lead, last, *rest):
    pieces, (b, h, e, own, o, f, sems) = rest[:-7], rest[-7:]
    cut = pieces[0].shape[0]
    loads = [
        pltpu.make_async_copy(inverse, own, sems.at[4]),
        pltpu.make_async_copy(history.at[1], h.at[1], sems.at[0]),
        pltpu.make_async_copy(blocks.at[1], b.at[1], sems.at[1]),
        pltpu.make_async_copy(history.at[0], h.at[0], sems.at[2]),
        pltpu.make_async_copy(blocks.at[0], b.at[0], sems.at[3]),
        pltpu.make_async_copy(excitation, e, sems.at[5]),
    ]
    for load in loads:
        load.start()
    nw, depth, _ = out.shape
    cw = depth - own.shape[0]
    loads[0].wait()
    for w in range(nw):
        o[w, cw:] = own[...]
    gathered = pl.ds(cw, own.shape[0])
    stores = [pltpu.make_async_copy(o.at[:, gathered], out.at[:, gathered], sems.at[6])]
    stores[-1].start()
    loads[1].wait()
    stores.append(pltpu.make_async_copy(h.at[1], last, sems.at[0]))
    stores[-1].start()
    loads[2].wait()
    total = mm(b[1], h[1])
    loads[3].wait()
    loads[4].wait()

    @pl.when(lax.axis_index(LAG) == 0)
    def _():
        for k, piece in enumerate(pieces):
            rows = b.at[0, (k + 1) * cut : (k + 2) * cut]
            pltpu.make_async_copy(rows, piece, sems.at[8 + k]).start()

    total = total + mm(b[0], h[0])
    loads[5].wait()
    total = less_field(total, e[0])
    for w in range(nw):
        o[w, :cw] = total[w * cw : (w + 1) * cw]
    summed = pl.ds(0, cw)
    stores.append(pltpu.make_async_copy(o.at[:, summed], out.at[:, summed], sems.at[4]))
    stores[-1].start()
    f[...] = less_field(jnp.zeros_like(e[1]), e[1])
    stores.append(pltpu.make_async_copy(f, lead, sems.at[7]))
    stores[-1].start()
    for store in stores:
        store.wait()

    @pl.when(lax.axis_index(LAG) == 0)
    def _():
        for k, piece in enumerate(pieces):
            rows = b.at[0, (k + 1) * cut : (k + 2) * cut]
            pltpu.make_async_copy(rows, piece, sems.at[8 + k]).wait()


def later_sums(blocks, before, history, out):
    out[...] = (mm(blocks[1], history[0]) + mm(blocks[0], before[...])).T


def second_step(got, blocks, *rest):
    sources, (out, piece, sem) = rest[:-3], rest[-3:]
    sources = (blocks.at[0, : piece.shape[0]], *sources)
    w = lax.axis_index(W)
    for k, source in zip(HOLDERS[:-1], sources):

        @pl.when(w == k)
        def _():
            pltpu.make_async_copy(source, piece, sem).start()

    @pl.when(functools.reduce(jnp.logical_and, [w != k for k in HOLDERS[:-1]]))
    def _():
        pltpu.make_async_copy(sources[-1], piece, sem).start()

    ny, depth, span = out.shape
    cw = (depth - piece.shape[0]) // 2
    high, low = parts(sum_first(got, 0, cw))
    for y in range(ny):
        out[y, :cw] = high
        out[y, cw : 2 * cw] = low
    pltpu.make_async_copy(sources[0], piece, sem).wait()
    for y in range(ny):
        out[y, 2 * cw :] = piece[:, y * span : (y + 1) * span]


def third_step(got, later, lead, out):
    nw = out.shape[0]
    cw = later.shape[0] // nw
    total = later[...] + lead[...]
    for w in range(nw):
        high, low = parts(total[w * cw : (w + 1) * cw])
        out[w, :cw] = high
        out[w, cw : 2 * cw] = low
        out[w, 2 * cw :] = got[0, 2 * cw :]


def fourth_step(got1, got2, got3, out, part1, first):
    nz, cw, rows = out.shape
    inverse = got1[:, cw:].reshape(-1, rows)
    term = -mm_t(sum_pairs(got2, 0, cw), inverse, lax.Precision.HIGHEST)
    for z in range(nz):
        out[z] = term
    part1[...] = sum_pairs(got3, 0, cw)
    cut = got3.shape[1] - 2 * cw
    for i, w in enumerate(HOLDERS):
        first[i * cut : (i + 1) * cut] = got3[w, 2 * cw :]


def fifth_step(got, part1, first, out, mine):
    value = sum_first(got, 0, got.shape[1])
    total = part1[...] + mm_t(value.astype(BF16), first[...])
    for y in range(out.shape[0]):
        out[y] = total
    cz = mine.shape[0]
    share = value[:cz]
    for z in range(1, value.shape[0] // cz):
        share = jnp.where(lax.axis_index("row") == z, value[z * cz : (z + 1) * cz], share)
    mine[...] = share


def sixth_step(got1, got, mine, out):
    cw = got.shape[1]
    inverse = got1[:, cw:].reshape(-1, got.shape[2])
    out[:cw] = -mm_t(sum_first(got, 0, cw), inverse, lax.Precision.HIGHEST)
    out[cw:] = mine[...]


def shards(blocks, history, excitation, self_inverse):
    ny, nx, nc, nz = (lax.axis_size(a) for a in ("y", "x", "core", "row"))
    nw = nx * nc
    rows, size = blocks.shape[1:]
    columns = history.shape[2]
    cw = columns // nw
    own = self_inverse.shape[0]
    nlag = ny * nw
    cut = rows // len(HOLDERS)
    span = nw * own
    work = 2 * rows * size * columns * 2
    small = 2 * cw * rows * span


    outs = [((nw, cw + own, rows), F32), ((columns, rows), F32), (history.shape[1:], BF16)]
    outs += [((cut, size), BF16)] * (len(HOLDERS) - 1)
    scratch = [pltpu.VMEM(blocks.shape, BF16), pltpu.VMEM(history.shape, BF16)]
    scratch += [pltpu.VMEM(excitation.shape, F32), pltpu.VMEM((own, rows), F32)]
    scratch += [pltpu.VMEM(*o) for o in outs[:2]] + [pltpu.SemaphoreType.DMA((7 + len(HOLDERS),))]
    args = blocks, history, excitation, self_inverse
    held, given = [pltpu.HBM] * len(args), [pltpu.HBM] * len(outs)
    send, lead, last, *pieces = call(
        first_sums, outs, work, *args, scratch=scratch, held=held, given=given, limit=60
    )
    before = lax.ppermute(last, LAG, [(i, i + 1) for i in range(nlag - 1)])
    got1 = swap(send, W)
    pieces = [lax.ppermute(p, LAG, [(0, w)]) for p, w in zip(pieces, HOLDERS[1:])]
    later = call(later_sums, ((columns, rows), F32), work, blocks, before, history)
    got1, later = lax.optimization_barrier((got1, later))
    send = call(
        second_step,
        ((ny, 2 * cw + cut, span), BF16),
        small,
        got1,
        blocks,
        *pieces,
        scratch=[pltpu.VMEM((cut, size), BF16), pltpu.SemaphoreType.DMA(())],
        held=[pltpu.VMEM] + [pltpu.HBM] * len(HOLDERS),
    )
    got2 = swap(send, "y")
    send = call(third_step, ((nw, 2 * cw + cut, rows), BF16), small, got2, later, lead)
    got3 = swap(send, W)
    outs = [((nz, cw, rows), F32), ((cw, rows), F32), ((rows, span), BF16)]
    send, part1, first = call(fourth_step, outs, small, got1, got2, got3)
    got4 = swap(send, "row")
    cz = cw // nz
    outs = [((ny, cw, rows), F32), ((cz, span), F32)]
    send, mine0 = call(fifth_step, outs, small, got4, part1, first)
    got5 = swap(send, "y")
    both = call(sixth_step, ((cw + cz, span), F32), small, got1, got5, mine0)
    both = both.reshape(cw + cz, nw, own).transpose(1, 0, 2).reshape(nw, 1, (cw + cz) * own)
    both = jnp.broadcast_to(both, (nw, nz, (cw + cz) * own)).reshape(nw * nz, (cw + cz) * own)
    got = swap(both, W + ("row",)).reshape(nw, nz, cw + cz, own)
    out1 = jnp.sum(got[:, :, :cw], axis=1).reshape(columns, own)
    out0 = got[:, :, cw:].reshape(columns, own)
    return jnp.stack([out0.T, out1.T])


def solution(mesh):
    n_row = mesh.shape["row"]
    fine = Mesh(np.asarray(mesh.devices).reshape(-1, 4, 2, n_row), ("y", "x", "core", "row"))
    return jax.shard_map(
        shards,
        mesh=fine,
        in_specs=(
            P(LAG, "row", None),
            P(LAG, None, None),
            P(None, "row", None),
            P(LAG, "row"),
        ),
        out_specs=P(None, LAG, None),
        check_vma=False,
    )
```

```python
import functools

import numpy as np
import jax
import jax.numpy as jnp
from jax import lax
from jax.experimental import pallas as pl
from jax.experimental.pallas import tpu as pltpu
from jax.sharding import Mesh, PartitionSpec as P

LAG = ("y", "x", "core")
W = ("x", "core")
HOLDERS = (0, 6, 2, 1)
F32 = jnp.float32
BF16 = jnp.bfloat16


def swap(pieces, axes):
    return lax.all_to_all(pieces, axes, 0, 0, tiled=True)


def call(body, outs, flops, *args, scratch=(), held=None, given=None, limit=24):
    single = not isinstance(outs, list)
    outs = [outs] if single else outs
    shapes = [jax.ShapeDtypeStruct(s, d) for s, d in outs]
    size = sum(a.size * a.dtype.itemsize for a in args)
    size += sum(s.size * s.dtype.itemsize for s in shapes)
    held = held or [pltpu.VMEM] * len(args)
    given = given or [pltpu.VMEM] * len(outs)
    specs = [pl.BlockSpec(memory_space=m) for m in given]
    return pl.pallas_call(
        body,
        out_shape=shapes[0] if single else shapes,
        in_specs=[pl.BlockSpec(memory_space=m) for m in held],
        out_specs=specs[0] if single else specs,
        scratch_shapes=scratch,
        cost_estimate=pl.CostEstimate(flops=flops, bytes_accessed=size, transcendentals=0),
        compiler_params=pltpu.CompilerParams(vmem_limit_bytes=limit * 1024 * 1024),
    )(*args)


def mm(left, right, precision=None):
    return jnp.dot(left, right, precision=precision, preferred_element_type=F32)


def mm_t(left, right, precision=None):
    return lax.dot_general(
        left, right, (((1,), (1,)), ((), ())), precision=precision, preferred_element_type=F32
    )


def parts(array):
    high = array.astype(BF16)
    return high, (array - high.astype(F32)).astype(BF16)


def sum_first(ref, start, stop):
    total = ref[0, start:stop].astype(F32)
    for i in range(1, ref.shape[0]):
        total = total + ref[i, start:stop].astype(F32)
    return total


def sum_pairs(ref, start, count):
    return sum_first(ref, start, start + count) + sum_first(ref, start + count, start + 2 * count)


def less_field(total, field):
    return jnp.where(lax.axis_index(LAG) == 0, total - field, total).T


def first_sums(blocks, history, excitation, inverse, out, lead, last, *rest):
    pieces, (b, h, e, own, o, f, sems) = rest[:-7], rest[-7:]
    cut = pieces[0].shape[0]
    loads = [
        pltpu.make_async_copy(inverse, own, sems.at[4]),
        pltpu.make_async_copy(history.at[1], h.at[1], sems.at[0]),
        pltpu.make_async_copy(blocks.at[1], b.at[1], sems.at[1]),
        pltpu.make_async_copy(history.at[0], h.at[0], sems.at[2]),
        pltpu.make_async_copy(blocks.at[0], b.at[0], sems.at[3]),
        pltpu.make_async_copy(excitation, e, sems.at[5]),
    ]
    for load in loads:
        load.start()
    nw, depth, _ = out.shape
    cw = depth - own.shape[0]
    loads[0].wait()
    for w in range(nw):
        o[w, cw:] = own[...]
    gathered = pl.ds(cw, own.shape[0])
    stores = [pltpu.make_async_copy(o.at[:, gathered], out.at[:, gathered], sems.at[6])]
    stores[-1].start()
    loads[1].wait()
    stores.append(pltpu.make_async_copy(h.at[1], last, sems.at[0]))
    stores[-1].start()
    loads[2].wait()
    total = mm(b[1], h[1])
    loads[3].wait()
    loads[4].wait()

    @pl.when(lax.axis_index(LAG) == 0)
    def _():
        for k, piece in enumerate(pieces):
            rows = b.at[0, (k + 1) * cut : (k + 2) * cut]
            pltpu.make_async_copy(rows, piece, sems.at[8 + k]).start()

    total = total + mm(b[0], h[0])
    loads[5].wait()
    total = less_field(total, e[0])
    for w in range(nw):
        o[w, :cw] = total[w * cw : (w + 1) * cw]
    summed = pl.ds(0, cw)
    stores.append(pltpu.make_async_copy(o.at[:, summed], out.at[:, summed], sems.at[4]))
    stores[-1].start()
    f[...] = less_field(jnp.zeros_like(e[1]), e[1])
    stores.append(pltpu.make_async_copy(f, lead, sems.at[7]))
    stores[-1].start()
    for store in stores:
        store.wait()

    @pl.when(lax.axis_index(LAG) == 0)
    def _():
        for k, piece in enumerate(pieces):
            rows = b.at[0, (k + 1) * cut : (k + 2) * cut]
            pltpu.make_async_copy(rows, piece, sems.at[8 + k]).wait()


def later_sums(blocks, before, history, out):
    out[...] = (mm(blocks[1], history[0]) + mm(blocks[0], before[...])).T


def second_step(got, blocks, *rest):
    sources, (out, piece, sem) = rest[:-3], rest[-3:]
    sources = (blocks.at[0, : piece.shape[0]], *sources)
    w = lax.axis_index(W)
    for k, source in zip(HOLDERS[:-1], sources):

        @pl.when(w == k)
        def _():
            pltpu.make_async_copy(source, piece, sem).start()

    @pl.when(functools.reduce(jnp.logical_and, [w != k for k in HOLDERS[:-1]]))
    def _():
        pltpu.make_async_copy(sources[-1], piece, sem).start()

    ny, depth, span = out.shape
    cw = (depth - piece.shape[0]) // 2
    high, low = parts(sum_first(got, 0, cw))
    for y in range(ny):
        out[y, :cw] = high
        out[y, cw : 2 * cw] = low
    pltpu.make_async_copy(sources[0], piece, sem).wait()
    for y in range(ny):
        out[y, 2 * cw :] = piece[:, y * span : (y + 1) * span]


def third_step(got, later, lead, out):
    nw = out.shape[0]
    cw = later.shape[0] // nw
    total = later[...] + lead[...]
    for w in range(nw):
        high, low = parts(total[w * cw : (w + 1) * cw])
        out[w, :cw] = high
        out[w, cw : 2 * cw] = low
        out[w, 2 * cw :] = got[0, 2 * cw :]


def fourth_step(got1, got2, got3, out, part1, first):
    nz, cw, rows = out.shape
    inverse = got1[:, cw:].reshape(-1, rows)
    term = -mm_t(sum_pairs(got2, 0, cw), inverse, lax.Precision.HIGHEST)
    for z in range(nz):
        out[z] = term
    part1[...] = sum_pairs(got3, 0, cw)
    cut = got3.shape[1] - 2 * cw
    for i, w in enumerate(HOLDERS):
        first[i * cut : (i + 1) * cut] = got3[w, 2 * cw :]


def fifth_step(got, part1, first, out, mine):
    value = sum_first(got, 0, got.shape[1])
    total = part1[...] + mm_t(value.astype(BF16), first[...])
    for y in range(out.shape[0]):
        out[y] = total
    cz = mine.shape[0]
    share = value[:cz]
    for z in range(1, value.shape[0] // cz):
        share = jnp.where(lax.axis_index("row") == z, value[z * cz : (z + 1) * cz], share)
    mine[...] = share


def sixth_step(got1, got, mine, out):
    cw = got.shape[1]
    inverse = got1[:, cw:].reshape(-1, got.shape[2])
    out[:cw] = -mm_t(sum_first(got, 0, cw), inverse, lax.Precision.HIGHEST)
    out[cw:] = mine[...]


def shards(blocks, history, excitation, self_inverse):
    ny, nx, nc, nz = (lax.axis_size(a) for a in ("y", "x", "core", "row"))
    nw = nx * nc
    rows, size = blocks.shape[1:]
    columns = history.shape[2]
    cw = columns // nw
    own = self_inverse.shape[0]
    nlag = ny * nw
    cut = rows // len(HOLDERS)
    span = nw * own
    work = 2 * rows * size * columns * 2
    small = 2 * cw * rows * span


    outs = [((nw, cw + own, rows), F32), ((columns, rows), F32), (history.shape[1:], BF16)]
    outs += [((cut, size), BF16)] * (len(HOLDERS) - 1)
    scratch = [pltpu.VMEM(blocks.shape, BF16), pltpu.VMEM(history.shape, BF16)]
    scratch += [pltpu.VMEM(excitation.shape, F32), pltpu.VMEM((own, rows), F32)]
    scratch += [pltpu.VMEM(*o) for o in outs[:2]] + [pltpu.SemaphoreType.DMA((7 + len(HOLDERS),))]
    args = blocks, history, excitation, self_inverse
    held, given = [pltpu.HBM] * len(args), [pltpu.HBM] * len(outs)
    send, lead, last, *pieces = call(
        first_sums, outs, work, *args, scratch=scratch, held=held, given=given, limit=60
    )
    before = lax.ppermute(last, LAG, [(i, i + 1) for i in range(nlag - 1)])
    got1 = swap(send, W)
    pieces = [lax.ppermute(p, LAG, [(0, w)]) for p, w in zip(pieces, HOLDERS[1:])]
    got1, before = lax.optimization_barrier((got1, before))
    later = call(later_sums, ((columns, rows), F32), work, blocks, before, history)
    got1, later = lax.optimization_barrier((got1, later))
    send = call(
        second_step,
        ((ny, 2 * cw + cut, span), BF16),
        small,
        got1,
        blocks,
        *pieces,
        scratch=[pltpu.VMEM((cut, size), BF16), pltpu.SemaphoreType.DMA(())],
        held=[pltpu.VMEM] + [pltpu.HBM] * len(HOLDERS),
    )
    got2 = swap(send, "y")
    send = call(third_step, ((nw, 2 * cw + cut, rows), BF16), small, got2, later, lead)
    got3 = swap(send, W)
    outs = [((nz, cw, rows), F32), ((cw, rows), F32), ((rows, span), BF16)]
    send, part1, first = call(fourth_step, outs, small, got1, got2, got3)
    got4 = swap(send, "row")
    cz = cw // nz
    outs = [((ny, cw, rows), F32), ((cz, span), F32)]
    send, mine0 = call(fifth_step, outs, small, got4, part1, first)
    got5 = swap(send, "y")
    both = call(sixth_step, ((cw + cz, span), F32), small, got1, got5, mine0)
    both = both.reshape(cw + cz, nw, own).transpose(1, 0, 2).reshape(nw, 1, (cw + cz) * own)
    both = jnp.broadcast_to(both, (nw, nz, (cw + cz) * own)).reshape(nw * nz, (cw + cz) * own)
    got = swap(both, W + ("row",)).reshape(nw, nz, cw + cz, own)
    out1 = jnp.sum(got[:, :, :cw], axis=1).reshape(columns, own)
    out0 = got[:, :, cw:].reshape(columns, own)
    return jnp.stack([out0.T, out1.T])


def solution(mesh):
    n_row = mesh.shape["row"]
    fine = Mesh(np.asarray(mesh.devices).reshape(-1, 4, 2, n_row), ("y", "x", "core", "row"))
    return jax.shard_map(
        shards,
        mesh=fine,
        in_specs=(
            P(LAG, "row", None),
            P(LAG, None, None),
            P(None, "row", None),
            P(LAG, "row"),
        ),
        out_specs=P(None, LAG, None),
        check_vma=False,
    )
```

```python
import functools

import numpy as np
import jax
import jax.numpy as jnp
from jax import lax
from jax.experimental import pallas as pl
from jax.experimental.pallas import tpu as pltpu
from jax.sharding import Mesh, PartitionSpec as P

LAG = ("y", "x", "core")
W = ("x", "core")
HOLDERS = (0, 1, 6, 2)
F32 = jnp.float32
BF16 = jnp.bfloat16


def swap(pieces, axes):
    return lax.all_to_all(pieces, axes, 0, 0, tiled=True)


def call(body, outs, flops, *args, scratch=(), held=None, given=None, limit=24):
    single = not isinstance(outs, list)
    outs = [outs] if single else outs
    shapes = [jax.ShapeDtypeStruct(s, d) for s, d in outs]
    size = sum(a.size * a.dtype.itemsize for a in args)
    size += sum(s.size * s.dtype.itemsize for s in shapes)
    held = held or [pltpu.VMEM] * len(args)
    given = given or [pltpu.VMEM] * len(outs)
    specs = [pl.BlockSpec(memory_space=m) for m in given]
    return pl.pallas_call(
        body,
        out_shape=shapes[0] if single else shapes,
        in_specs=[pl.BlockSpec(memory_space=m) for m in held],
        out_specs=specs[0] if single else specs,
        scratch_shapes=scratch,
        cost_estimate=pl.CostEstimate(flops=flops, bytes_accessed=size, transcendentals=0),
        compiler_params=pltpu.CompilerParams(vmem_limit_bytes=limit * 1024 * 1024),
    )(*args)


def mm(left, right, precision=None):
    return jnp.dot(left, right, precision=precision, preferred_element_type=F32)


def mm_t(left, right, precision=None):
    return lax.dot_general(
        left, right, (((1,), (1,)), ((), ())), precision=precision, preferred_element_type=F32
    )


def parts(array):
    high = array.astype(BF16)
    return high, (array - high.astype(F32)).astype(BF16)


def sum_first(ref, start, stop):
    total = ref[0, start:stop].astype(F32)
    for i in range(1, ref.shape[0]):
        total = total + ref[i, start:stop].astype(F32)
    return total


def sum_pairs(ref, start, count):
    return sum_first(ref, start, start + count) + sum_first(ref, start + count, start + 2 * count)


def less_field(total, field):
    return jnp.where(lax.axis_index(LAG) == 0, total - field, total).T


def first_sums(blocks, history, excitation, inverse, out, lead, last, *rest):
    pieces, (b, h, e, own, o, f, sems) = rest[:-7], rest[-7:]
    cut = pieces[0].shape[0]
    loads = [
        pltpu.make_async_copy(inverse, own, sems.at[4]),
        pltpu.make_async_copy(history.at[1], h.at[1], sems.at[0]),
        pltpu.make_async_copy(blocks.at[1], b.at[1], sems.at[1]),
        pltpu.make_async_copy(history.at[0], h.at[0], sems.at[2]),
        pltpu.make_async_copy(blocks.at[0], b.at[0], sems.at[3]),
        pltpu.make_async_copy(excitation, e, sems.at[5]),
    ]
    for load in loads:
        load.start()
    nw, depth, _ = out.shape
    cw = depth - own.shape[0]
    loads[0].wait()
    for w in range(nw):
        o[w, cw:] = own[...]
    gathered = pl.ds(cw, own.shape[0])
    stores = [pltpu.make_async_copy(o.at[:, gathered], out.at[:, gathered], sems.at[6])]
    stores[-1].start()
    loads[1].wait()
    stores.append(pltpu.make_async_copy(h.at[1], last, sems.at[0]))
    stores[-1].start()
    loads[2].wait()
    total = mm(b[1], h[1])
    loads[3].wait()
    loads[4].wait()

    @pl.when(lax.axis_index(LAG) == 0)
    def _():
        for k, piece in enumerate(pieces):
            rows = b.at[0, (k + 1) * cut : (k + 2) * cut]
            pltpu.make_async_copy(rows, piece, sems.at[8 + k]).start()

    total = total + mm(b[0], h[0])
    loads[5].wait()
    total = less_field(total, e[0])
    for w in range(nw):
        o[w, :cw] = total[w * cw : (w + 1) * cw]
    summed = pl.ds(0, cw)
    stores.append(pltpu.make_async_copy(o.at[:, summed], out.at[:, summed], sems.at[4]))
    stores[-1].start()
    f[...] = less_field(jnp.zeros_like(e[1]), e[1])
    stores.append(pltpu.make_async_copy(f, lead, sems.at[7]))
    stores[-1].start()
    for store in stores:
        store.wait()

    @pl.when(lax.axis_index(LAG) == 0)
    def _():
        for k, piece in enumerate(pieces):
            rows = b.at[0, (k + 1) * cut : (k + 2) * cut]
            pltpu.make_async_copy(rows, piece, sems.at[8 + k]).wait()


def later_sums(blocks, before, history, out):
    out[...] = (mm(blocks[1], history[0]) + mm(blocks[0], before[...])).T


def second_step(got, blocks, *rest):
    sources, (out, piece, sem) = rest[:-3], rest[-3:]
    sources = (blocks.at[0, : piece.shape[0]], *sources)
    w = lax.axis_index(W)
    for k, source in zip(HOLDERS[:-1], sources):

        @pl.when(w == k)
        def _():
            pltpu.make_async_copy(source, piece, sem).start()

    @pl.when(functools.reduce(jnp.logical_and, [w != k for k in HOLDERS[:-1]]))
    def _():
        pltpu.make_async_copy(sources[-1], piece, sem).start()

    ny, depth, span = out.shape
    cw = (depth - piece.shape[0]) // 2
    high, low = parts(sum_first(got, 0, cw))
    for y in range(ny):
        out[y, :cw] = high
        out[y, cw : 2 * cw] = low
    pltpu.make_async_copy(sources[0], piece, sem).wait()
    for y in range(ny):
        out[y, 2 * cw :] = piece[:, y * span : (y + 1) * span]


def third_step(got, later, lead, out):
    nw = out.shape[0]
    cw = later.shape[0] // nw
    total = later[...] + lead[...]
    for w in range(nw):
        high, low = parts(total[w * cw : (w + 1) * cw])
        out[w, :cw] = high
        out[w, cw : 2 * cw] = low
        out[w, 2 * cw :] = got[0, 2 * cw :]


def fourth_step(got1, got2, got3, out, part1, first):
    nz, cw, rows = out.shape
    inverse = got1[:, cw:].reshape(-1, rows)
    term = -mm_t(sum_pairs(got2, 0, cw), inverse, lax.Precision.HIGHEST)
    for z in range(nz):
        out[z] = term
    part1[...] = sum_pairs(got3, 0, cw)
    cut = got3.shape[1] - 2 * cw
    for i, w in enumerate(HOLDERS):
        first[i * cut : (i + 1) * cut] = got3[w, 2 * cw :]


def fifth_step(got, part1, first, out, mine):
    value = sum_first(got, 0, got.shape[1])
    total = part1[...] + mm_t(value.astype(BF16), first[...])
    for y in range(out.shape[0]):
        out[y] = total
    cz = mine.shape[0]
    share = value[:cz]
    for z in range(1, value.shape[0] // cz):
        share = jnp.where(lax.axis_index("row") == z, value[z * cz : (z + 1) * cz], share)
    mine[...] = share


def sixth_step(got1, got, mine, out):
    cw = got.shape[1]
    inverse = got1[:, cw:].reshape(-1, got.shape[2])
    out[:cw] = -mm_t(sum_first(got, 0, cw), inverse, lax.Precision.HIGHEST)
    out[cw:] = mine[...]


def shards(blocks, history, excitation, self_inverse):
    ny, nx, nc, nz = (lax.axis_size(a) for a in ("y", "x", "core", "row"))
    nw = nx * nc
    rows, size = blocks.shape[1:]
    columns = history.shape[2]
    cw = columns // nw
    own = self_inverse.shape[0]
    nlag = ny * nw
    cut = rows // len(HOLDERS)
    span = nw * own
    work = 2 * rows * size * columns * 2
    small = 2 * cw * rows * span


    outs = [((nw, cw + own, rows), F32), ((columns, rows), F32), (history.shape[1:], BF16)]
    outs += [((cut, size), BF16)] * (len(HOLDERS) - 1)
    scratch = [pltpu.VMEM(blocks.shape, BF16), pltpu.VMEM(history.shape, BF16)]
    scratch += [pltpu.VMEM(excitation.shape, F32), pltpu.VMEM((own, rows), F32)]
    scratch += [pltpu.VMEM(*o) for o in outs[:2]] + [pltpu.SemaphoreType.DMA((7 + len(HOLDERS),))]
    args = blocks, history, excitation, self_inverse
    held, given = [pltpu.HBM] * len(args), [pltpu.HBM] * len(outs)
    send, lead, last, *pieces = call(
        first_sums, outs, work, *args, scratch=scratch, held=held, given=given, limit=60
    )
    before = lax.ppermute(last, LAG, [(i, i + 1) for i in range(nlag - 1)])
    got1 = swap(send, W)
    pieces = [lax.ppermute(p, LAG, [(0, w)]) for p, w in zip(pieces, HOLDERS[1:])]
    later = call(later_sums, ((columns, rows), F32), work, blocks, before, history)
    got1, later = lax.optimization_barrier((got1, later))
    send = call(
        second_step,
        ((ny, 2 * cw + cut, span), BF16),
        small,
        got1,
        blocks,
        *pieces,
        scratch=[pltpu.VMEM((cut, size), BF16), pltpu.SemaphoreType.DMA(())],
        held=[pltpu.VMEM] + [pltpu.HBM] * len(HOLDERS),
    )
    got2 = swap(send, "y")
    send = call(third_step, ((nw, 2 * cw + cut, rows), BF16), small, got2, later, lead)
    got3 = swap(send, W)
    outs = [((nz, cw, rows), F32), ((cw, rows), F32), ((rows, span), BF16)]
    send, part1, first = call(fourth_step, outs, small, got1, got2, got3)
    got4 = swap(send, "row")
    cz = cw // nz
    outs = [((ny, cw, rows), F32), ((cz, span), F32)]
    send, mine0 = call(fifth_step, outs, small, got4, part1, first)
    got5 = swap(send, "y")
    both = call(sixth_step, ((cw + cz, span), F32), small, got1, got5, mine0)
    both = both.reshape(cw + cz, nw, own).transpose(1, 0, 2).reshape(nw, 1, (cw + cz) * own)
    both = jnp.broadcast_to(both, (nw, nz, (cw + cz) * own)).reshape(nw * nz, (cw + cz) * own)
    got = swap(both, W + ("row",)).reshape(nw, nz, cw + cz, own)
    out1 = jnp.sum(got[:, :, :cw], axis=1).reshape(columns, own)
    out0 = got[:, :, cw:].reshape(columns, own)
    return jnp.stack([out0.T, out1.T])


def solution(mesh):
    n_row = mesh.shape["row"]
    fine = Mesh(np.asarray(mesh.devices).reshape(-1, 4, 2, n_row), ("y", "x", "core", "row"))
    return jax.shard_map(
        shards,
        mesh=fine,
        in_specs=(
            P(LAG, "row", None),
            P(LAG, None, None),
            P(None, "row", None),
            P(LAG, "row"),
        ),
        out_specs=P(None, LAG, None),
        check_vma=False,
    )
```
